32 devices in a mesh: cam: 16 (over z, x, core), depth: 2 (over y).
Axes of the slice: x: 2, y: 2, z: 4, core: 2. Of those that a mesh axis runs over, the one named last changes fastest.
Arguments:
- features: bfloat16 [16, 32, 8, 512], P('cam'), may hold values from -6 to 6
- view_mask: int32 [16, 4], P('cam'), may hold values 0 or 1
- row_offset: int32 [16, 4, 8], P('cam', None, 'depth'), may hold values from 0 to 3
- frac_row: float32 [16, 4, 8], P('cam', None, 'depth'), may hold values from 0 to 1
- col_offset: int32 [16, 4, 8], P('cam', None, 'depth'), may hold values from -32 to 32
- frac_col: float32 [16, 4, 8], P('cam', None, 'depth'), may hold values from 0 to 1
- first_kernel: bfloat16 [8, 32, 3, 3, 3], replicated, may hold values from -0.21875 to 0.21875
- first_bias: float32 [8], replicated, may hold values from -0.5 to 0.5
- second_kernel: bfloat16 [8, 8, 3, 3, 3], replicated, may hold values from -0.4375 to 0.4375
- cotangent: bfloat16 [16, 8, 8, 4, 512], P('cam', None, 'depth'), may hold values from -6 to 6
Outputs:
- feature_grad: float32 [16, 32, 8, 512], P('cam', 'depth')
- first_grad: float32 [8, 32, 3, 3, 3], replicated
- second_grad: float32 [8, 8, 3, 3, 3], replicated
The draws below stay inside these ranges and needn't reach their ends.
All inputs are finite; a program needn't handle non-finite values. No bound on the sum of `view_mask` on one device may be relied on, other than what follows from the above.
Results may differ from the reference program's by a relative error of at most 0.0053.
Values may be sent and summed in bfloat16 or wider, within the bound.
A program may use at most 128 MiB of HBM per device.

```python
import jax
import jax.numpy as jnp
from jax import lax

C = 32
K = 8
W = 512
D = 8
H = 4
SPAN = 4
SHIFT = 32
HS = 8
NCAM = 16


def set_ends(array, rng, smallest, high):
    spot = [jax.random.randint(jax.random.fold_in(rng, axis), (), 0, length) for axis, length in enumerate(array.shape)]
    widest = array.shape.index(max(array.shape))
    neighbour = spot[:widest] + [(spot[widest] + 1) % array.shape[widest]] + spot[widest + 1:]
    return array.at[tuple(spot)].set(smallest).at[tuple(neighbour)].set(high)


def steps_of(rng, shape, pieces, low, top_value):
    level = 1.0
    for dim, shards_of in pieces:
        draws = jax.random.uniform(jax.random.fold_in(jax.random.fold_in(rng, 6), dim), (shards_of,), jnp.float32, low / len(pieces), top_value / len(pieces))
        level = level * jnp.repeat(jnp.exp(draws), shape[dim] // shards_of).reshape((-1,) + (1,) * (len(shape) - 1 - dim))
    return level


def scatter_about(stream_key, dims, width, reach, shards=(), kind=jnp.bfloat16):
    gain = steps_of(stream_key, dims, shards, -0.22, 0.18) if shards else 1.0
    result = jax.random.normal(stream_key, dims, jnp.float32) * width * gain
    return jnp.minimum(jnp.maximum(result, -reach), reach).astype(kind)


def setup_inputs(seed: int = 0) -> dict:
    key_list = jax.random.split(jax.random.key(seed), 11)
    return {
        "features": scatter_about(key_list[0], (NCAM, C, HS, W), 1.0, 6.0, ((0, 16),)),
        "view_mask": set_ends((jax.random.randint(key_list[1], (NCAM, 4), 0, 4) < 3).astype(jnp.int32), jax.random.fold_in(key_list[1], 1), 0, 1),
        "row_offset": set_ends(jax.random.randint(key_list[2], (NCAM, 4, D), 0, SPAN), jax.random.fold_in(key_list[2], 1), 0, SPAN - 1).astype(jnp.int32),
        "frac_row": jnp.clip(1.0 * jax.random.uniform(key_list[3], (NCAM, 4, D), jnp.float32) ** steps_of(key_list[3], (NCAM, 4, D), ((0, 16), (2, 2)), -0.2, 0.2), 0.0, 1.0),
        "col_offset": set_ends(jax.random.randint(key_list[4], (NCAM, 4, D), -SHIFT, SHIFT + 1), jax.random.fold_in(key_list[4], 1), -SHIFT, SHIFT).astype(jnp.int32),
        "frac_col": jnp.clip(1.0 * jax.random.uniform(key_list[5], (NCAM, 4, D), jnp.float32) ** steps_of(key_list[5], (NCAM, 4, D), ((0, 16), (2, 2)), -0.2, 0.2), 0.0, 1.0),
        "first_kernel": scatter_about(key_list[6], (K, C, 3, 3, 3), (27 * C) ** -0.5, 0.21875),
        "first_bias": jnp.clip(jax.random.uniform(key_list[7], (K,), jnp.float32, -0.5, 0.5), -0.5, 0.5),
        "second_kernel": scatter_about(key_list[8], (K, K, 3, 3, 3), (27 * K) ** -0.5, 0.4375),
        "cotangent": scatter_about(key_list[9], (NCAM, K, D, H, W), 1.0, 6.0, ((0, 16), (2, 2))),
    }


view_offsets = (-2, -1, 1, 2)

def conv_same(volume, kernel, depth_pad):
    return lax.conv_general_dilated(volume[None], kernel, (1, 1, 1), [depth_pad, (1, 1), (1, 1)], dimension_numbers=('NCDHW', 'OIDHW', 'NCDHW'), preferred_element_type=jnp.float32)[0]

def flipped(kernel):
    return jnp.transpose(jnp.flip(kernel, (2, 3, 4)), (1, 0, 2, 3, 4))

def silu_slope(value):
    gate = jax.nn.sigmoid(value)
    return gate * (1.0 + value * (1.0 - gate))

def pad_source(src_band):
    return jnp.pad(src_band.astype(jnp.float32), ((0, 0), (0, 0), (SHIFT, SHIFT + 1)))

def plane_warp(padded, row_start, col_start, frac_r, frac_c):
    window = lax.dynamic_slice(padded, (jnp.zeros((), jnp.int32), row_start.astype(jnp.int32), (col_start + SHIFT).astype(jnp.int32)), (padded.shape[0], H + 1, W + 1))
    row_mixed = (1.0 - frac_r) * window[:, :H, :] + frac_r * window[:, 1:, :]
    return (1.0 - frac_c) * row_mixed[:, :, :W] + frac_c * row_mixed[:, :, 1:]

def slot_warp(padded, row_starts, col_starts, fracs_r, fracs_c):
    return jax.vmap(plane_warp, in_axes=(None, 0, 0, 0, 0), out_axes=1)(padded, row_starts, col_starts, fracs_r, fracs_c)

def weight_term(volume, grad_out):
    widened = volume.astype(jnp.float32)

    def convolve(kernel):
        return lax.conv_general_dilated(widened[None], kernel, (1, 1, 1), [(1, 1), (1, 1), (1, 1)], dimension_numbers=('NCDHW', 'OIDHW', 'NCDHW'), precision=lax.Precision.HIGHEST)[0]
    start_kernel = jnp.zeros((grad_out.shape[0], volume.shape[0], 3, 3, 3), jnp.float32)
    outcome, pullback = jax.vjp(convolve, start_kernel)
    return pullback(grad_out.astype(jnp.float32))[0]

def reference(features, view_mask, row_offset, frac_row, col_offset, frac_col, first_kernel, first_bias, second_kernel, cotangent):
    top_row = SPAN // 2

    def per_camera(carried, camera):
        grad_total, grad_first, grad_second = carried
        own_band = features[camera]
        reference_view = own_band[:, top_row:top_row + H, :].astype(jnp.float32)[:, None]
        view_weights = view_mask[camera].astype(jnp.float32)
        view_count = 1.0 + jnp.sum(view_weights)
        first_moment = reference_view
        second_moment = reference_view * reference_view
        paddings, warps, owners = ([], [], [])
        for slot_id in range(4):
            owner = (camera + view_offsets[slot_id]) % NCAM
            padded = pad_source(features[owner])
            warped = slot_warp(padded, row_offset[camera, slot_id], col_offset[camera, slot_id], frac_row[camera, slot_id], frac_col[camera, slot_id])
            first_moment = first_moment + view_weights[slot_id] * warped
            second_moment = second_moment + view_weights[slot_id] * (warped * warped)
            paddings.append(padded)
            warps.append(warped)
            owners.append(owner)
        view_mean = first_moment / view_count
        cost_volume = (second_moment / view_count - view_mean * view_mean).astype(jnp.bfloat16)
        pre_act = conv_same(cost_volume, first_kernel, (1, 1)) + first_bias[:, None, None, None]
        hidden = jax.nn.silu(pre_act).astype(jnp.bfloat16)
        cot_camera = cotangent[camera]
        hidden_grad = conv_same(cot_camera, flipped(second_kernel), (1, 1))
        pre_grad = (hidden_grad * silu_slope(pre_act)).astype(jnp.bfloat16)
        cost_grad = conv_same(pre_grad, flipped(first_kernel), (1, 1))
        grad_first = grad_first + weight_term(cost_volume, pre_grad)
        grad_second = grad_second + weight_term(hidden, cot_camera)
        scaled = 2.0 * cost_grad / view_count
        ref_grad = lax.optimization_barrier(jnp.sum(scaled * (reference_view - view_mean), axis=1))
        grad_total = grad_total.at[camera].add(jnp.pad(ref_grad, ((0, 0), (top_row, SPAN - top_row), (0, 0))))
        for slot_id in range(4):
            slot_grad = view_weights[slot_id] * scaled * (warps[slot_id] - view_mean)
            outcome, pullback = jax.vjp(lambda padded_src: slot_warp(padded_src, row_offset[camera, slot_id], col_offset[camera, slot_id], frac_row[camera, slot_id], frac_col[camera, slot_id]), paddings[slot_id])
            source_grad = pullback(slot_grad)[0][:, :, SHIFT:SHIFT + W]
            grad_total = grad_total.at[owners[slot_id]].add(source_grad)
        return ((grad_total, grad_first, grad_second), None)
    initial = (jnp.zeros(features.shape, jnp.float32), jnp.zeros(first_kernel.shape, jnp.float32), jnp.zeros(second_kernel.shape, jnp.float32))
    finals, outcome = lax.scan(per_camera, initial, jnp.arange(NCAM, dtype=jnp.int32))
    grad_scale = (NCAM * D * H * W) ** (-0.5)
    return (finals[0], finals[1] * grad_scale, finals[2] * grad_scale)
```

```python
import functools

import jax
import jax.numpy as jnp
from jax import lax
from jax.experimental import pallas as pl
from jax.experimental.pallas import tpu as pltpu
from jax.sharding import PartitionSpec as P

SHIFT = 32
view_offsets = (-2, -1, 1, 2)
SMEM = pl.BlockSpec(memory_space=pltpu.SMEM)
VMEM = pl.BlockSpec(memory_space=pltpu.VMEM)


def banded(kernel, height):
    taps = jnp.transpose(kernel, (4, 0, 2, 3, 1))
    zero = jnp.zeros((), kernel.dtype)
    rows = []
    for h in range(height):
        rows.append(lax.pad(taps, zero, [(0, 0, 0)] * 3 + [(h - 1, height - 2 - h, 0)] + [(0, 0, 0)]))
    return jnp.stack(rows, axis=1)


def flipped(kernel):
    return jnp.transpose(jnp.flip(kernel, (2, 3, 4)), (1, 0, 2, 3, 4))


def mul(a, b):
    return jnp.dot(a, b, preferred_element_type=jnp.float32)


def mul_t(a, b):
    return lax.dot_general(a, b, (((1,), (1,)), ((), ())), preferred_element_type=jnp.float32)


def lanes(width):
    return lax.broadcasted_iota(jnp.int32, (1, width), 1)


def from_left(x):
    width = x.shape[1]
    return jnp.where(lanes(width) > 0, pltpu.roll(x, 1, 1), 0.0)


def from_right(x):
    width = x.shape[1]
    return jnp.where(lanes(width) < width - 1, pltpu.roll(x, width - 1, 1), 0.0)


def compute(
    dims,
    row_ref, col_ref, fy_ref, fx_ref, m_ref, inv_ref,
    feat_ref, cot_ref, b1_ref, b2_ref, b3_ref, bias_ref,
    grad_ref, wsum_ref,
    warp, mean, cost, scot, spre, pre_acc, hid, acc1, acc2, cg,
):
    chans, mid, height, width, own, planes, top = dims
    band = height * chans
    mband = height * mid
    first_own = (planes - own) * lax.axis_index("depth")
    inv = inv_ref[0]

    def weights(s, p):
        c = col_ref[s, p]
        fx = fx_ref[s, p]
        at = lanes(width) + c
        left = jnp.where((at >= 0) & (at < width), 1.0 - fx, 0.0)
        right = jnp.where((at >= -1) & (at < width - 1), fx, 0.0)
        return c, left, right

    for end in (0, planes + 1):
        scot[end * 3 * mband : (end + 1) * 3 * mband, :] = jnp.zeros((3 * mband, width), scot.dtype)
        spre[end * 3 * mband : (end + 1) * 3 * mband, :] = jnp.zeros((3 * mband, width), spre.dtype)
        cost[end * band : (end + 1) * band, :] = jnp.zeros((band, width), cost.dtype)
    for p in range(planes):
        plane = cot_ref[p * mband : (p + 1) * mband, :]
        wide = plane.astype(jnp.float32)
        base = (p + 1) * 3 * mband
        scot[base : base + mband, :] = from_left(wide).astype(scot.dtype)
        scot[base + mband : base + 2 * mband, :] = plane
        scot[base + 2 * mband : base + 3 * mband, :] = from_right(wide).astype(scot.dtype)

    def warp_plane(p, _):
        for h in range(height):
            ref = feat_ref[0, (top + h) * chans : (top + h + 1) * chans, :].astype(jnp.float32)
            first = ref
            second = ref * ref
            for s in range(4):
                c, left, right = weights(s, p)
                fy = fy_ref[s, p]
                start = pl.multiple_of((row_ref[s, p] + h) * chans, chans)
                upper = feat_ref[s + 1, pl.ds(start, chans), :].astype(jnp.float32)
                start = pl.multiple_of((row_ref[s, p] + h + 1) * chans, chans)
                lower = feat_ref[s + 1, pl.ds(start, chans), :].astype(jnp.float32)
                mixed = (1.0 - fy) * upper + fy * lower
                here = pltpu.roll(mixed, jnp.where(c > 0, width - c, -c), 1)
                after = pltpu.roll(here, width - 1, 1)
                warped = left * here + right * after
                warp[s, p, h * chans : (h + 1) * chans, :] = warped
                weighted = m_ref[s] * warped
                first = first + weighted
                second = second + weighted * warped
            average = first * inv
            mean[p, h * chans : (h + 1) * chans, :] = average
            at = pl.multiple_of((p + 1) * band + h * chans, chans)
            cost[pl.ds(at, chans), :] = (second * inv - average * average).astype(cost.dtype)
        return 0

    lax.fori_loop(0, planes, warp_plane, 0)

    def middle(i, _):
        p = first_own // 2 + i
        x = cost[pl.ds(pl.multiple_of(p * band, band), 3 * band), :]
        parts = mul(b1_ref[...], x)
        pre = from_left(parts[:mband]) + parts[mband : 2 * mband] + from_right(parts[2 * mband :])
        pre = pre + bias_ref[...]
        gate = jax.nn.sigmoid(pre)
        hid[pl.ds(pl.multiple_of(p * mband, mband), mband), :] = (pre * gate).astype(hid.dtype)
        y = scot[pl.ds(pl.multiple_of(p * 3 * mband, 3 * mband), 3 * 3 * mband), :]
        back = mul(b2_ref[...], y) * (gate * (1.0 + pre * (1.0 - gate)))
        base = pl.multiple_of((p + 1) * 3 * mband, mband)
        spre[pl.ds(base, mband), :] = from_left(back).astype(spre.dtype)
        spre[pl.ds(base + mband, mband), :] = back.astype(spre.dtype)
        spre[pl.ds(base + 2 * mband, mband), :] = from_right(back).astype(spre.dtype)
        return 0

    lax.fori_loop(0, own + (planes - own) // 2, middle, 0)

    grad_ref[...] = jnp.zeros_like(grad_ref)
    acc1[...] = jnp.zeros_like(acc1)
    acc2[...] = jnp.zeros_like(acc2)

    def back_plane(i, _):
        p = first_own + i
        s3 = spre[pl.ds(pl.multiple_of(p * 3 * mband, 3 * mband), 9 * mband), :]
        c3 = scot[pl.ds(pl.multiple_of(p * 3 * mband, 3 * mband), 9 * mband), :]
        cg[...] = mul(b3_ref[...], s3) * (2.0 * inv)
        acc1[...] += mul_t(s3, cost[pl.ds(pl.multiple_of((p + 1) * band, band), band), :])
        acc2[:, :mband] += mul_t(c3, hid[pl.ds(pl.multiple_of(p * mband, mband), mband), :])
        for h in range(height):
            rows = slice(h * chans, (h + 1) * chans)
            ref = feat_ref[0, (top + h) * chans : (top + h + 1) * chans, :].astype(jnp.float32)
            grad_ref[0, (top + h) * chans : (top + h + 1) * chans, :] += cg[rows, :] * (ref - mean[p, rows, :])
        for s in range(4):
            c, left, right = weights(s, p)
            fy = fy_ref[s, p]
            turn = jnp.where(c < 0, width + c, c)
            carried = None
            for h in range(height + 1):
                if h < height:
                    rows = slice(h * chans, (h + 1) * chans)
                    grad = (m_ref[s] * cg[rows, :]) * (warp[s, p, rows, :] - mean[p, rows, :])
                    spread = pltpu.roll(left * grad + pltpu.roll(right * grad, 1, 1), turn, 1)
                    value = (1.0 - fy) * spread
                    if carried is not None:
                        value = value + carried
                    carried = fy * spread
                else:
                    value = carried
                start = pl.multiple_of((row_ref[s, p] + h) * chans, chans)
                grad_ref[s + 1, pl.ds(start, chans), :] += value
        return 0

    lax.fori_loop(0, own, back_plane, 0)

    def fold(acc, block, offset):
        rows = acc[...].reshape(9, height, mid, 128)
        lane = lax.broadcasted_iota(jnp.int32, (1, 1, 128), 2)
        total = None
        for g in range(height):
            ok = (lane >= (g - 1) * block) & (lane < (g + 2) * block) & (lane < height * block)
            part = jnp.where(ok, rows[:, g], 0.0).reshape(9 * mid, 128)
            turn = (offset - (g - 1) * block) % 128
            if turn:
                part = pltpu.roll(part, turn, 1)
            total = part if total is None else total + part
        return total

    wsum_ref[...] = fold(acc1, chans, 0) + fold(acc2, mid, 3 * chans)


def shards(
    features, view_mask, row_offset, frac_row, col_offset, frac_col,
    first_kernel, first_bias, second_kernel, cotangent,
):
    cams, slabs = lax.axis_size("cam"), lax.axis_size("depth")
    _, chans, held, width = features.shape
    mid = first_kernel.shape[0]
    _, _, own, height, _ = cotangent.shape
    top = (held - height) // 2
    band, mband = height * chans, height * mid
    assert slabs == 2 and own >= 2 and band == 128
    planes = own + 2
    me = lax.axis_index("depth")
    swap = [(0, 1), (1, 0)]

    own_band = jnp.transpose(features[0], (1, 0, 2)).reshape(held * chans, width)
    bands = [own_band]
    for offset in view_offsets:
        bands.append(lax.ppermute(own_band, "cam", [((i + offset) % cams, i) for i in range(cams)]))
    feat = jnp.stack(bands)

    def widened(x, axis):
        edge = lax.dynamic_slice_in_dim(x, (own - 2) * (1 - me), 2, axis)
        other = lax.ppermute(edge, "depth", swap)
        return jnp.where(
            me == 0, jnp.concatenate([x, other], axis), jnp.concatenate([other, x], axis)
        )

    cot = jnp.transpose(cotangent[0], (1, 2, 0, 3)).reshape(own, mband, width)
    cot = widened(cot, 0).reshape(planes * mband, width)
    scalars = jnp.stack(
        [row_offset[0].astype(jnp.float32), col_offset[0].astype(jnp.float32), frac_row[0], frac_col[0]]
    )
    scalars = widened(scalars, 2)
    mask = view_mask[0].astype(jnp.float32)
    inv = (1.0 / (1.0 + jnp.sum(mask))).reshape(1)

    b1 = banded(first_kernel, height).reshape(3 * mband, 3 * band)
    b2 = jnp.transpose(banded(flipped(second_kernel), height), (1, 2, 3, 0, 4, 5)).reshape(mband, 9 * mband)
    b3 = jnp.transpose(banded(flipped(first_kernel), height), (1, 2, 3, 0, 4, 5)).reshape(band, 9 * mband)
    bias = jnp.tile(first_bias, height).reshape(mband, 1)

    f32, bf16 = jnp.float32, jnp.bfloat16
    grads, wsum = pl.pallas_call(
        functools.partial(compute, (chans, mid, height, width, own, planes, top)),
        out_shape=(
            jax.ShapeDtypeStruct((5, held * chans, width), f32),
            jax.ShapeDtypeStruct((9 * mid, 128), f32),
        ),
        in_specs=[SMEM] * 6 + [VMEM] * 6,
        out_specs=(VMEM, VMEM),
        scratch_shapes=[
            pltpu.VMEM((4, planes, band, width), f32),
            pltpu.VMEM((planes, band, width), f32),
            pltpu.VMEM(((planes + 2) * band, width), bf16),
            pltpu.VMEM(((planes + 2) * 3 * mband, width), bf16),
            pltpu.VMEM(((planes + 2) * 3 * mband, width), bf16),
            pltpu.VMEM((8, 128), f32),
            pltpu.VMEM((planes * mband, width), bf16),
            pltpu.VMEM((9 * mband, 128), f32),
            pltpu.VMEM((9 * mband, 128), f32),
            pltpu.VMEM((band, width), f32),
        ],
        compiler_params=pltpu.CompilerParams(vmem_limit_bytes=40 * 2**20),
        name="core",
    )(
        scalars[0].astype(jnp.int32), scalars[1].astype(jnp.int32), scalars[2], scalars[3], mask, inv,
        feat, cot, b1, b2, b3, bias,
    )

    grads = grads.reshape(5, held, chans, width)
    part = lax.psum_scatter(grads, "depth", scatter_dimension=2, tiled=True)
    summed = part[0]
    for s, offset in enumerate(view_offsets):
        summed = summed + lax.ppermute(part[s + 1], "cam", [(i, (i + offset) % cams) for i in range(cams)])
    feature_grad = jnp.transpose(summed, (1, 0, 2))
    wsum = lax.psum(wsum, ("cam", "depth"))
    scale = (cams * slabs * own * height * width) ** (-0.5)
    taps = (wsum * scale).reshape(3, 3, mid, 128)[::-1, ::-1]
    first = taps[..., : 3 * chans].reshape(3, 3, mid, 3, chans)
    second = taps[..., 3 * chans : 3 * chans + 3 * mid].reshape(3, 3, mid, 3, mid)
    order = (2, 4, 0, 3, 1)
    return feature_grad[None], jnp.transpose(first, order), jnp.transpose(second, order)


def solution(mesh):
    placed = (
        P("cam", None, None, None),
        P("cam", None),
        P("cam", None, "depth"),
        P("cam", None, "depth"),
        P("cam", None, "depth"),
        P("cam", None, "depth"),
        P(),
        P(),
        P(),
        P("cam", None, "depth", None, None),
    )
    return jax.shard_map(
        shards,
        mesh=mesh,
        in_specs=placed,
        out_specs=(P("cam", "depth", None, None), P(), P()),
        check_vma=False,
    )
```

```python
import functools

import jax
import jax.numpy as jnp
from jax import lax
from jax.experimental import pallas as pl
from jax.experimental.pallas import tpu as pltpu
from jax.sharding import PartitionSpec as P

SHIFT = 32
view_offsets = (-2, -1, 1, 2)
MESH = pl.DeviceIdType.MESH
VMEM = pl.BlockSpec(memory_space=pltpu.VMEM)


def banded(kernel, height):
    taps = jnp.transpose(kernel, (4, 0, 2, 3, 1))
    zero = jnp.zeros((), kernel.dtype)
    rows = []
    for h in range(height):
        rows.append(lax.pad(taps, zero, [(0, 0, 0)] * 3 + [(h - 1, height - 2 - h, 0)] + [(0, 0, 0)]))
    return jnp.stack(rows, axis=1)


def flipped(kernel):
    return jnp.transpose(jnp.flip(kernel, (2, 3, 4)), (1, 0, 2, 3, 4))


def mul(a, b):
    return jnp.dot(a, b, preferred_element_type=jnp.float32)


def mul_t(a, b):
    return lax.dot_general(a, b, (((1,), (1,)), ((), ())), preferred_element_type=jnp.float32)


def lanes(width):
    return lax.broadcasted_iota(jnp.int32, (1, width), 1)


def from_left(x):
    width = x.shape[1]
    return jnp.where(lanes(width) > 0, pltpu.roll(x, 1, 1), 0.0)


def from_right(x):
    width = x.shape[1]
    return jnp.where(lanes(width) < width - 1, pltpu.roll(x, width - 1, 1), 0.0)


SMALL = 64


def turned(x, by):
    count, width = x.shape
    parts = []
    for start in range(0, width, 256):
        before = (start - 128) % width
        after = (start + 256) % width
        parts.append(
            jnp.concatenate(
                [x[:, before : before + 128], x[:, start : start + 256], x[:, after : after + 128]], axis=1
            )
        )
    source = lax.broadcasted_iota(jnp.int32, (512, 256), 0) - 128
    target = lax.broadcasted_iota(jnp.int32, (512, 256), 1)
    pick = jnp.where(source - target == by, 1.0, 0.0).astype(x.dtype)
    out = mul(jnp.concatenate(parts, axis=0), pick)
    return jnp.concatenate([out[i * count : (i + 1) * count] for i in range(width // 256)], axis=1)


def compute(
    dims,
    feat_ref, cot_ref, ints_ref, floats_ref, b1_ref, b2_ref, b3_ref, bias_ref,
    grad_ref, wsum_ref,
    bands, halo, ints_in, floats_in, ints, floats,
    warp, mean, cost, scot, spre, hid, acc1, acc2, cg, pad, taps,
    own_grad, out_grad, a_send, a_recv, b_send, b_recv, c_send, c_recv, ar, ar_in,
    send_sem, recv_sem, local_sem,
):
    chans, mid, height, held, width, own, planes, cams = dims
    top = (held - height) // 2
    lead = held - height - 1
    half = chans // 2
    band = height * chans
    mband = height * mid
    steps = ar_in.shape[0]

    cam = lax.axis_index("cam")
    me = lax.axis_index("depth")
    other = 1 - me
    first_own = (planes - own) * me
    odd = lax.rem(cam, 2)

    def at(offset):
        return lax.rem(cam + cams + offset * (2 * odd - 1), cams)

    def slot(t):
        return t + odd * (3 - 2 * t)

    mate = at(-1)
    partners = []
    reach = 1
    while reach < cams:
        bit = lax.rem(cam // reach, 2)
        partners.append((cam + reach * (1 - 2 * bit), me))
        reach *= 2
    partners.append((cam, other))

    barrier = pltpu.get_barrier_semaphore()
    greeted = [(at(-2), me), (at(-1), me), (at(1), me), (at(2), me)] + partners
    for device in greeted:
        pl.semaphore_signal(barrier, inc=1, device_id=device, device_id_type=MESH)
    pl.semaphore_wait(barrier, len(greeted))

    started = []

    def remote(n, src, dst, device):
        return pltpu.make_async_remote_copy(
            src_ref=src, dst_ref=dst, send_sem=send_sem.at[n], recv_sem=recv_sem.at[n],
            device_id=device, device_id_type=MESH,
        )

    def begin(copy):
        copy.start()
        started.append(copy)
        return copy

    edge = pl.multiple_of((own - 2) * other * mband, mband)
    ints_copy = begin(remote(0, ints_ref, ints_in, (cam, other)))
    floats_copy = begin(remote(1, floats_ref, floats_in, (cam, other)))
    feat1 = begin(remote(4, feat_ref, bands.at[1], (at(1), me)))
    feat2 = begin(remote(5, feat_ref, bands.at[2], (mate, me)))
    halo_copy = begin(remote(2, cot_ref.at[pl.ds(edge, 2 * mband), :], halo, (cam, other)))
    feat0 = begin(remote(3, feat_ref, bands.at[0], (at(-2), me)))
    own_ints = pltpu.make_async_copy(ints_ref, ints.at[me], local_sem.at[0])
    own_floats = pltpu.make_async_copy(floats_ref, floats.at[me], local_sem.at[1])
    own_ints.start()
    own_floats.start()

    for end in (0, planes + 1):
        scot[end * 3 * mband : (end + 1) * 3 * mband, :] = jnp.zeros((3 * mband, width), scot.dtype)
        spre[end * 3 * mband : (end + 1) * 3 * mband, :] = jnp.zeros((3 * mband, width), spre.dtype)
        cost[end * band : (end + 1) * band, :] = jnp.zeros((band, width), cost.dtype)

    def shift_plane(plane, p):
        wide = plane.astype(jnp.float32)
        base = pl.multiple_of((p + 1) * 3 * mband, mband)
        scot[pl.ds(base, mband), :] = from_left(wide).astype(scot.dtype)
        scot[pl.ds(base + mband, mband), :] = plane
        scot[pl.ds(base + 2 * mband, mband), :] = from_right(wide).astype(scot.dtype)

    for i in range(own):
        shift_plane(cot_ref[i * mband : (i + 1) * mband, :], first_own + i)

    own_ints.wait()
    own_floats.wait()
    ints_copy.wait_recv()
    floats_copy.wait_recv()
    more_ints = pltpu.make_async_copy(ints_in, ints.at[other], local_sem.at[2])
    more_floats = pltpu.make_async_copy(floats_in, floats.at[other], local_sem.at[3])
    more_ints.start()
    more_floats.start()
    halo_copy.wait_recv()
    for i in range(2):
        shift_plane(halo[i * mband : (i + 1) * mband, :], own * other + i)
    more_ints.wait()
    more_floats.wait()

    inv = floats[me, 4, SMALL]

    def place(p):
        at_plane = p + me * (2 * own - planes)
        return at_plane // own, lax.rem(at_plane, own)

    def row_of(s, p):
        slab, lane = place(p)
        return ints[slab, s, lane]

    def weights(s, p):
        slab, lane = place(p)
        c = ints[slab, s + 4, lane]
        fy = floats[slab, s, lane]
        fx = floats[slab, s + 4, lane]
        spot = lanes(width) + c
        left = jnp.where((spot >= 0) & (spot < width), 1.0 - fx, 0.0)
        right = jnp.where((spot >= -1) & (spot < width - 1), fx, 0.0)
        return c, fy, left, right

    def warp_slot(t, last):
        s = slot(t)

        def plane(p, _):
            c, fy, left, right = weights(s, p)
            r = row_of(s, p)
            window = bands[t, : band + chans, :]
            for k in range(1, lead + 1):
                window = jnp.where(r == k, bands[t, k * chans : band + (k + 1) * chans, :], window)
            here = turned(window, c)
            for h in range(height):
                rows = slice(h * chans, (h + 1) * chans)
                mixed = (1.0 - fy) * here[rows] + fy * here[(h + 1) * chans : (h + 2) * chans]
                warped = left * mixed + right * pltpu.roll(mixed, width - 1, 1)
                warp[t, p, rows, :] = warped
                if last:
                    ref = feat_ref[(top + h) * chans : (top + h + 1) * chans, :].astype(jnp.float32)
                    first = ref
                    second = ref * ref
                    for u in range(4):
                        view = warped if u == t else warp[u, p, rows, :]
                        weighted = floats[me, slot(u), SMALL] * view
                        first = first + weighted
                        second = second + weighted * view
                    average = first * inv
                    mean[p, rows, :] = average
                    spot = pl.multiple_of((p + 1) * band + h * chans, chans)
                    cost[pl.ds(spot, chans), :] = (second * inv - average * average).astype(cost.dtype)
            return 0

        lax.fori_loop(0, planes, plane, 0)

    feat2.wait_recv()
    warp_slot(2, False)
    feat1.wait_recv()
    feat3 = begin(remote(6, bands.at[1], bands.at[3], (mate, me)))
    warp_slot(1, False)
    feat3.wait_recv()
    warp_slot(3, False)
    feat0.wait_recv()
    warp_slot(0, True)

    def middle(i, _):
        p = first_own // 2 + i
        x = cost[pl.ds(pl.multiple_of(p * band, band), 3 * band), :]
        parts = mul(b1_ref[...], x)
        pre = from_left(parts[:mband]) + parts[mband : 2 * mband] + from_right(parts[2 * mband :])
        pre = pre + bias_ref[...]
        gate = jax.nn.sigmoid(pre)
        hid[pl.ds(pl.multiple_of(p * mband, mband), mband), :] = (pre * gate).astype(hid.dtype)
        y = scot[pl.ds(pl.multiple_of(p * 3 * mband, 3 * mband), 3 * 3 * mband), :]
        back = mul(b2_ref[...], y) * (gate * (1.0 + pre * (1.0 - gate)))
        base = pl.multiple_of((p + 1) * 3 * mband, mband)
        spre[pl.ds(base, mband), :] = from_left(back).astype(spre.dtype)
        spre[pl.ds(base + mband, mband), :] = back.astype(spre.dtype)
        spre[pl.ds(base + 2 * mband, mband), :] = from_right(back).astype(spre.dtype)
        return 0

    lax.fori_loop(0, own + (planes - own) // 2, middle, 0)

    acc1[...] = jnp.zeros_like(acc1)
    acc2[...] = jnp.zeros_like(acc2)
    own_grad[...] = jnp.zeros_like(own_grad)

    def back_plane(i, _):
        p = first_own + i
        s3 = spre[pl.ds(pl.multiple_of(p * 3 * mband, 3 * mband), 9 * mband), :]
        c3 = scot[pl.ds(pl.multiple_of(p * 3 * mband, 3 * mband), 9 * mband), :]
        cg[i] = mul(b3_ref[...], s3) * (2.0 * inv)
        acc1[...] += mul_t(s3, cost[pl.ds(pl.multiple_of((p + 1) * band, band), band), :])
        acc2[:, :mband] += mul_t(c3, hid[pl.ds(pl.multiple_of(p * mband, mband), mband), :])
        return 0

    lax.fori_loop(0, own, back_plane, 0)

    def fold(acc, block, offset):
        rows = acc[...].reshape(9, height, mid, 128)
        lane = lax.broadcasted_iota(jnp.int32, (1, 1, 128), 2)
        total = None
        for g in range(height):
            ok = (lane >= (g - 1) * block) & (lane < (g + 2) * block) & (lane < height * block)
            part = jnp.where(ok, rows[:, g], 0.0).reshape(9 * mid, 128)
            turn = (offset - (g - 1) * block) % 128
            if turn:
                part = pltpu.roll(part, turn, 1)
            total = part if total is None else total + part
        return total

    ar[0] = fold(acc1, chans, 0) + fold(acc2, mid, 3 * chans)
    reduce_copies = []

    def reduce_begin():
        k = len(reduce_copies)
        if k < steps:
            reduce_copies.append(begin(remote(14 + k, ar.at[k], ar_in.at[k], partners[k])))

    def reduce_next():
        k = len(reduce_copies)
        if k <= steps and k > 0:
            reduce_copies[k - 1].wait_recv()
            ar[k] = ar[k - 1] + ar_in[k - 1]

    reduce_begin()

    def slot_back(t, emit):
        s = slot(t)
        weight = floats[me, s, SMALL]

        def plane(i, _):
            p = first_own + i
            c, fy, left, right = weights(s, p)
            carried = None
            for h in range(height):
                rows = slice(h * chans, (h + 1) * chans)
                grad = (weight * cg[i, rows, :]) * (warp[t, p, rows, :] - mean[p, rows, :])
                taps[rows, :] = (left * grad + pltpu.roll(right * grad, 1, 1)).astype(taps.dtype)
            spread = turned(taps[...], -c)
            for h in range(height):
                rows = slice(h * chans, (h + 1) * chans)
                value = (1.0 - fy) * spread[rows]
                if carried is not None:
                    value = value + carried
                carried = fy * spread[rows]
                pad[i, rows, :] = value
            pad[i, height * chans :, :] = carried
            return 0

        lax.fori_loop(0, own, plane, 0)
        starts = [row_of(s, first_own + i) for i in range(own)]
        for r in range(held):
            total = None
            for i in range(own):
                part = jnp.zeros((chans, width), pad.dtype)
                for k in range(lead + 1):
                    if 0 <= r - k <= height:
                        row = pad[i, (r - k) * chans : (r - k + 1) * chans, :]
                        part = jnp.where(starts[i] == k, row, part)
                total = part if total is None else total + part
            for e in range(2):
                emit(e, slice(r * half, (r + 1) * half), total[e * half : (e + 1) * half])

    def to_mate(n):
        def emit(e, rows, value):
            a_send[n, e, rows, :] = value.astype(a_send.dtype)

        return emit

    def outward(n):
        def emit(e, rows, value):
            out_grad[n, e, rows, :] = value

        return emit

    slot_back(3, to_mate(1))
    a1 = begin(remote(8, a_send.at[1], a_recv.at[1], (mate, me)))
    reduce_next()
    reduce_begin()
    slot_back(2, to_mate(0))
    a0 = begin(remote(7, a_send.at[0], a_recv.at[0], (mate, me)))
    reduce_next()
    reduce_begin()
    slot_back(0, outward(0))
    b_send[0] = out_grad[0, other].astype(b_send.dtype)
    b0 = begin(remote(9, b_send.at[0], b_recv.at[0], (cam, other)))
    reduce_next()
    reduce_begin()
    slot_back(1, outward(1))
    a1.wait_recv()
    b_send[1] = (out_grad[1, other] + a_recv[1, other].astype(jnp.float32)).astype(b_send.dtype)
    b1 = begin(remote(10, b_send.at[1], b_recv.at[1], (cam, other)))
    reduce_next()
    reduce_begin()

    for h in range(height):
        rows = slice(h * chans, (h + 1) * chans)
        ref = feat_ref[(top + h) * chans : (top + h + 1) * chans, :].astype(jnp.float32)
        total = None
        for i in range(own):
            part = cg[i, rows, :] * (ref - mean[first_own + i, rows, :])
            total = part if total is None else total + part
        for e in range(2):
            own_grad[e, (top + h) * half : (top + h + 1) * half, :] = total[e * half : (e + 1) * half]
    a0.wait_recv()
    b_send[2] = (own_grad[other] + a_recv[0, other].astype(jnp.float32)).astype(b_send.dtype)
    b2 = begin(remote(11, b_send.at[2], b_recv.at[2], (cam, other)))

    b0.wait_recv()
    c_send[0] = (out_grad[0, me] + b_recv[0].astype(jnp.float32)).astype(c_send.dtype)
    c0 = begin(remote(12, c_send.at[0], c_recv.at[0], (at(2), me)))
    b1.wait_recv()
    c_send[1] = (
        out_grad[1, me] + a_recv[1, me].astype(jnp.float32) + b_recv[1].astype(jnp.float32)
    ).astype(c_send.dtype)
    c1 = begin(remote(13, c_send.at[1], c_recv.at[1], (at(1), me)))
    while len(reduce_copies) < steps:
        reduce_next()
        reduce_begin()
    reduce_next()
    wsum_ref[...] = ar[steps]
    b2.wait_recv()
    own_grad[me] = own_grad[me] + a_recv[0, me].astype(jnp.float32) + b_recv[2].astype(jnp.float32)
    c0.wait_recv()
    c1.wait_recv()
    grad_ref[...] = own_grad[me] + (c_recv[0].astype(jnp.float32) + c_recv[1].astype(jnp.float32))
    for copy in started:
        copy.wait_send()


def shards(
    features, view_mask, row_offset, frac_row, col_offset, frac_col,
    first_kernel, first_bias, second_kernel, cotangent,
):
    cams, slabs = lax.axis_size("cam"), lax.axis_size("depth")
    _, chans, held, width = features.shape
    mid = first_kernel.shape[0]
    _, _, own, height, _ = cotangent.shape
    band, mband, half = height * chans, height * mid, chans // 2
    assert slabs == 2 and 2 <= own <= 64 and band == 128 and width % 256 == 0 and cams & (cams - 1) == 0
    planes = own + 2
    steps = cams.bit_length()

    feat = jnp.transpose(features[0], (1, 0, 2)).reshape(held * chans, width)
    cot = jnp.transpose(cotangent[0], (1, 2, 0, 3)).reshape(own * mband, width)
    mask = view_mask[0].astype(jnp.float32)
    inv = 1.0 / (1.0 + jnp.sum(mask))
    wide = ((0, 0), (0, SMALL - own))
    ints = jnp.pad(jnp.concatenate([row_offset[0], col_offset[0]]), ((0, 0), (0, 128 - own)))
    small = jnp.concatenate([mask, jnp.broadcast_to(inv, (4,))])[:, None]
    floats = jnp.concatenate(
        [
            jnp.pad(jnp.concatenate([frac_row[0], frac_col[0]]), wide),
            jnp.pad(small, ((0, 0), (0, 127 - SMALL))),
        ],
        axis=1,
    )

    b1 = banded(first_kernel, height).reshape(3 * mband, 3 * band)
    b2 = jnp.transpose(banded(flipped(second_kernel), height), (1, 2, 3, 0, 4, 5)).reshape(mband, 9 * mband)
    b3 = jnp.transpose(banded(flipped(first_kernel), height), (1, 2, 3, 0, 4, 5)).reshape(band, 9 * mband)
    bias = jnp.tile(first_bias, height).reshape(mband, 1)

    f32, bf16, i32 = jnp.float32, jnp.bfloat16, jnp.int32
    rows = held * half
    grads, wsum = pl.pallas_call(
        functools.partial(compute, (chans, mid, height, held, width, own, planes, cams)),
        out_shape=(
            jax.ShapeDtypeStruct((rows, width), f32),
            jax.ShapeDtypeStruct((9 * mid, 128), f32),
        ),
        in_specs=[VMEM] * 8,
        out_specs=(VMEM, VMEM),
        scratch_shapes=[
            pltpu.VMEM((4, held * chans, width), bf16),
            pltpu.VMEM((2 * mband, width), bf16),
            pltpu.VMEM((8, 128), i32),
            pltpu.VMEM((8, 128), f32),
            pltpu.SMEM((2, 8, 128), i32),
            pltpu.SMEM((2, 8, 128), f32),
            pltpu.VMEM((4, planes, band, width), f32),
            pltpu.VMEM((planes, band, width), f32),
            pltpu.VMEM(((planes + 2) * band, width), bf16),
            pltpu.VMEM(((planes + 2) * 3 * mband, width), bf16),
            pltpu.VMEM(((planes + 2) * 3 * mband, width), bf16),
            pltpu.VMEM((planes * mband, width), bf16),
            pltpu.VMEM((9 * mband, 128), f32),
            pltpu.VMEM((9 * mband, 128), f32),
            pltpu.VMEM((own, band, width), f32),
            pltpu.VMEM((own, band + chans, width), f32),
            pltpu.VMEM((band, width), bf16),
            pltpu.VMEM((2, rows, width), f32),
            pltpu.VMEM((2, 2, rows, width), f32),
            pltpu.VMEM((2, 2, rows, width), bf16),
            pltpu.VMEM((2, 2, rows, width), bf16),
            pltpu.VMEM((3, rows, width), bf16),
            pltpu.VMEM((3, rows, width), bf16),
            pltpu.VMEM((2, rows, width), bf16),
            pltpu.VMEM((2, rows, width), bf16),
            pltpu.VMEM((steps + 1, 9 * mid, 128), f32),
            pltpu.VMEM((steps, 9 * mid, 128), f32),
            pltpu.SemaphoreType.DMA((14 + steps,)),
            pltpu.SemaphoreType.DMA((14 + steps,)),
            pltpu.SemaphoreType.DMA((4,)),
        ],
        compiler_params=pltpu.CompilerParams(
            vmem_limit_bytes=48 * 2**20, collective_id=0, has_side_effects=True
        ),
        name="core",
    )(feat, cot, ints, floats, b1, b2, b3, bias)

    feature_grad = jnp.transpose(grads.reshape(held, half, width), (1, 0, 2))
    scale = (cams * slabs * own * height * width) ** (-0.5)
    taps = (wsum * scale).reshape(3, 3, mid, 128)[::-1, ::-1]
    first = taps[..., : 3 * chans].reshape(3, 3, mid, 3, chans)
    second = taps[..., 3 * chans : 3 * chans + 3 * mid].reshape(3, 3, mid, 3, mid)
    order = (2, 4, 0, 3, 1)
    return feature_grad[None], jnp.transpose(first, order), jnp.transpose(second, order)


def solution(mesh):
    placed = (
        P("cam", None, None, None),
        P("cam", None),
        P("cam", None, "depth"),
        P("cam", None, "depth"),
        P("cam", None, "depth"),
        P("cam", None, "depth"),
        P(),
        P(),
        P(),
        P("cam", None, "depth", None, None),
    )
    return jax.shard_map(
        shards,
        mesh=mesh,
        in_specs=placed,
        out_specs=(P("cam", "depth", None, None), P(), P()),
        check_vma=False,
    )
```

```python
import functools

import jax
import jax.numpy as jnp
from jax import lax
from jax.experimental import pallas as pl
from jax.experimental.pallas import tpu as pltpu
from jax.sharding import PartitionSpec as P

view_offsets = (-2, -1, 1, 2)
MESH = pl.DeviceIdType.MESH
SMEM = pl.BlockSpec(memory_space=pltpu.SMEM)
VMEM = pl.BlockSpec(memory_space=pltpu.VMEM)


def mul(a, b):
    return jnp.dot(a, b, preferred_element_type=jnp.float32)


def mul_t(a, b):
    return lax.dot_general(a, b, (((1,), (1,)), ((), ())), preferred_element_type=jnp.float32)


def lanes(width):
    return lax.broadcasted_iota(jnp.int32, (1, width), 1)


def from_left(x):
    width = x.shape[1]
    return jnp.where(lanes(width) > 0, pltpu.roll(x, 1, 1), 0.0)


def from_right(x):
    width = x.shape[1]
    return jnp.where(lanes(width) < width - 1, pltpu.roll(x, width - 1, 1), 0.0)


def turned(x, by):
    count, width = x.shape
    parts = []
    for start in range(0, width, 256):
        before = (start - 128) % width
        after = (start + 256) % width
        parts.append(
            jnp.concatenate(
                [x[:, before : before + 128], x[:, start : start + 256], x[:, after : after + 128]], axis=1
            )
        )
    source = lax.broadcasted_iota(jnp.int32, (512, 256), 0) - 128
    target = lax.broadcasted_iota(jnp.int32, (512, 256), 1)
    pick = jnp.where(source - target == by, 1.0, 0.0).astype(x.dtype)
    out = mul(jnp.concatenate(parts, axis=0), pick)
    return jnp.concatenate([out[i * count : (i + 1) * count] for i in range(width // 256)], axis=1)


def compute(
    dims,
    raw_ref, cotangent_ref, ints_ref, floats_ref, mask_ref, bias_ref, w1_ref, w2_ref,
    grad_ref, wsum_ref,
    bands, halo, ints_in, floats_in, ints, floats,
    warp, mean, cost, scot, spre, hid, acc1, acc2, cg, pad, taps,
    own_grad, out_grad, a_send, a_recv, b_send, b_recv, c_send, c_recv, ar, ar_in,
    wide, cot_wide, feat_ref, cot_ref, b1_ref, b1_wide, b2_ref, b2_wide, b3_ref, b3_wide, bias,
    send_sem, recv_sem, local_sem,
):
    chans, mid, height, held, width, own, planes, cams = dims
    top = (held - height) // 2
    lead = held - height - 1
    half = chans // 2
    band = height * chans
    mband = height * mid
    steps = ar_in.shape[0]

    cam = lax.axis_index("cam")
    me = lax.axis_index("depth")
    other = 1 - me
    first_own = (planes - own) * me
    odd = lax.rem(cam, 2)

    def at(offset):
        return lax.rem(cam + cams + offset * (2 * odd - 1), cams)

    def slot(t):
        return t + odd * (3 - 2 * t)

    mate = at(-1)
    partners = []
    reach = 1
    while reach < cams:
        bit = lax.rem(cam // reach, 2)
        partners.append((cam + reach * (1 - 2 * bit), me))
        reach *= 2
    partners.append((cam, other))

    barrier = pltpu.get_barrier_semaphore()
    greeted = [(at(-2), me), (at(-1), me), (at(1), me), (at(2), me)] + partners
    for device in greeted:
        pl.semaphore_signal(barrier, inc=1, device_id=device, device_id_type=MESH)

    wide[...] = raw_ref[...].astype(jnp.float32)
    for r in range(held):
        feat_ref[r * chans : (r + 1) * chans, :] = wide[:, r, :].astype(feat_ref.dtype)

    pl.semaphore_wait(barrier, len(greeted))

    started = []

    def remote(n, src, dst, device):
        return pltpu.make_async_remote_copy(
            src_ref=src, dst_ref=dst, send_sem=send_sem.at[n], recv_sem=recv_sem.at[n],
            device_id=device, device_id_type=MESH,
        )

    def begin(copy):
        copy.start()
        started.append(copy)
        return copy

    span = held // 2 * chans

    def part(ref, e):
        return ref.at[pl.ds(pl.multiple_of(e * span, span), span), :]

    feat1 = begin(remote(4, part(feat_ref, me), part(bands.at[1], me), (at(1), me)))
    feat0 = begin(remote(3, part(feat_ref, me), part(bands.at[0], me), (at(-2), me)))
    feat2 = begin(remote(5, feat_ref, bands.at[2], (mate, me)))
    ints_copy = begin(remote(0, ints_ref, ints_in, (cam, other)))
    floats_copy = begin(remote(1, floats_ref, floats_in, (cam, other)))
    own_ints = pltpu.make_async_copy(ints_ref, ints.at[me], local_sem.at[0])
    own_floats = pltpu.make_async_copy(floats_ref, floats.at[me], local_sem.at[1])
    own_ints.start()
    own_floats.start()

    for i in range(own):
        cot_wide[:, i * height : (i + 1) * height, :] = cotangent_ref[:, i].astype(jnp.float32)
    for i in range(own):
        cot_ref[i * mband : (i + 1) * mband, :] = jnp.concatenate(
            [cot_wide[:, i * height + h, :] for h in range(height)], axis=0
        ).astype(cot_ref.dtype)
    edge = pl.multiple_of((own - 2) * other * mband, mband)
    halo_copy = begin(remote(2, cot_ref.at[pl.ds(edge, 2 * mband), :], halo, (cam, other)))

    for end in (0, planes + 1):
        scot[end * 3 * mband : (end + 1) * 3 * mband, :] = jnp.zeros((3 * mband, width), scot.dtype)
        spre[end * 3 * mband : (end + 1) * 3 * mband, :] = jnp.zeros((3 * mband, width), spre.dtype)
        cost[end * band : (end + 1) * band, :] = jnp.zeros((band, width), cost.dtype)

    def shift_plane(plane, p):
        wide = plane.astype(jnp.float32)
        base = pl.multiple_of((p + 1) * 3 * mband, mband)
        scot[pl.ds(base, mband), :] = from_left(wide).astype(scot.dtype)
        scot[pl.ds(base + mband, mband), :] = plane
        scot[pl.ds(base + 2 * mband, mband), :] = from_right(wide).astype(scot.dtype)

    for i in range(own):
        shift_plane(cot_ref[i * mband : (i + 1) * mband, :], first_own + i)

    def blocks(w_ref, block, kd, kw):
        taps = []
        for kh in range(3):
            tap = w_ref[kd, kh, kw].astype(jnp.float32)
            taps.append(jnp.concatenate([tap, jnp.zeros((mid, 128 - block), jnp.float32)], axis=1))
        found = []
        for h in range(height):
            total = None
            for kh in range(3):
                to = h + kh - 1
                if 0 <= to < height:
                    moved = taps[kh] if to == 0 else pltpu.roll(taps[kh], to * block, 1)
                    total = moved if total is None else total + moved
            found.append(total)
        return found

    for kd in range(3):
        for kw in range(3):
            for h, value in enumerate(blocks(w1_ref, chans, kd, kw)):
                row = (kw * height + h) * mid
                b1_wide[row : row + mid, kd * 128 : (kd + 1) * 128] = value
                row = (((2 - kd) * 3 + 2 - kw) * height + h) * mid
                b3_wide[row : row + mid, :] = value
            for h, value in enumerate(blocks(w2_ref, mid, kd, kw)):
                row = (((2 - kd) * 3 + 2 - kw) * height + h) * mid
                b2_wide[row : row + mid, :] = value
    for ref in (b2_wide, b3_wide):
        ref[9 * mband :, :] = jnp.zeros((ref.shape[0] - 9 * mband, 128), jnp.float32)
    b1_ref[...] = b1_wide[...].astype(b1_ref.dtype)
    b2_ref[...] = jnp.transpose(b2_wide[...])[:mband].astype(b2_ref.dtype)
    b3_ref[...] = jnp.transpose(b3_wide[...]).astype(b3_ref.dtype)
    which = lax.rem(lax.broadcasted_iota(jnp.int32, (mband, width), 0), mid)
    column = jnp.zeros((mband, width), jnp.float32)
    for o in range(mid):
        column = jnp.where(which == o, bias_ref[o], column)
    bias[...] = column

    def weight_of(s):
        return mask_ref[s].astype(jnp.float32)

    count = 1.0 + weight_of(0) + weight_of(1) + weight_of(2) + weight_of(3)
    inv = 1.0 / jnp.full((1, width), count, jnp.float32)

    own_ints.wait()
    own_floats.wait()
    ints_copy.wait_recv()
    floats_copy.wait_recv()
    more_ints = pltpu.make_async_copy(ints_in, ints.at[other], local_sem.at[2])
    more_floats = pltpu.make_async_copy(floats_in, floats.at[other], local_sem.at[3])
    more_ints.start()
    more_floats.start()
    halo_copy.wait_recv()
    for i in range(2):
        shift_plane(halo[i * mband : (i + 1) * mband, :], own * other + i)
    more_ints.wait()
    more_floats.wait()

    def place(p):
        at_plane = p + me * (2 * own - planes)
        return at_plane // own, lax.rem(at_plane, own)

    def row_of(s, p):
        slab, lane = place(p)
        return ints[slab, s, lane]

    def weights(s, p):
        slab, lane = place(p)
        c = ints[slab, s + 4, lane]
        fy = floats[slab, s, lane]
        fx = floats[slab, s + 4, lane]
        spot = lanes(width) + c
        left = jnp.where((spot >= 0) & (spot < width), 1.0 - fx, 0.0)
        right = jnp.where((spot >= -1) & (spot < width - 1), fx, 0.0)
        return c, fy, left, right

    def warp_slot(t, last):
        s = slot(t)

        def plane(p, _):
            c, fy, left, right = weights(s, p)
            r = row_of(s, p)
            window = bands[t, : band + chans, :]
            for k in range(1, lead + 1):
                window = jnp.where(r == k, bands[t, k * chans : band + (k + 1) * chans, :], window)
            here = turned(window, c)
            for h in range(height):
                rows = slice(h * chans, (h + 1) * chans)
                mixed = (1.0 - fy) * here[rows] + fy * here[(h + 1) * chans : (h + 2) * chans]
                warped = left * mixed + right * pltpu.roll(mixed, width - 1, 1)
                warp[t, p, rows, :] = warped
                if last:
                    ref = feat_ref[(top + h) * chans : (top + h + 1) * chans, :].astype(jnp.float32)
                    first = ref
                    second = ref * ref
                    for u in range(4):
                        view = warped if u == t else warp[u, p, rows, :]
                        weighted = weight_of(slot(u)) * view
                        first = first + weighted
                        second = second + weighted * view
                    average = first * inv
                    mean[p, rows, :] = average
                    spot = pl.multiple_of((p + 1) * band + h * chans, chans)
                    cost[pl.ds(spot, chans), :] = (second * inv - average * average).astype(cost.dtype)
            return 0

        lax.fori_loop(0, planes, plane, 0)

    feat2.wait_recv()
    warp_slot(2, False)
    feat1.wait_recv()
    over1 = begin(remote(14, part(bands.at[1], me), part(bands.at[1], me), (cam, other)))
    feat3 = begin(remote(6, part(bands.at[1], me), part(bands.at[3], me), (mate, me)))
    feat0.wait_recv()
    over0 = begin(remote(15, part(bands.at[0], me), part(bands.at[0], me), (cam, other)))
    over1.wait_recv()
    over3 = begin(remote(16, part(bands.at[1], other), part(bands.at[3], other), (mate, me)))
    warp_slot(1, False)
    feat3.wait_recv()
    over3.wait_recv()
    warp_slot(3, False)
    over0.wait_recv()
    warp_slot(0, True)

    def middle(i, _):
        p = first_own // 2 + i
        x = cost[pl.ds(pl.multiple_of(p * band, band), 3 * band), :]
        parts = mul(b1_ref[...], x)
        pre = from_left(parts[:mband]) + parts[mband : 2 * mband] + from_right(parts[2 * mband :])
        pre = pre + bias[...]
        gate = jax.nn.sigmoid(pre)
        hid[pl.ds(pl.multiple_of(p * mband, mband), mband), :] = (pre * gate).astype(hid.dtype)
        y = scot[pl.ds(pl.multiple_of(p * 3 * mband, 3 * mband), 3 * 3 * mband), :]
        back = mul(b2_ref[:, : 9 * mband], y) * (gate * (1.0 + pre * (1.0 - gate)))
        base = pl.multiple_of((p + 1) * 3 * mband, mband)
        spre[pl.ds(base, mband), :] = from_left(back).astype(spre.dtype)
        spre[pl.ds(base + mband, mband), :] = back.astype(spre.dtype)
        spre[pl.ds(base + 2 * mband, mband), :] = from_right(back).astype(spre.dtype)
        return 0

    lax.fori_loop(0, own + (planes - own) // 2, middle, 0)

    acc1[...] = jnp.zeros_like(acc1)
    acc2[...] = jnp.zeros_like(acc2)
    own_grad[...] = jnp.zeros_like(own_grad)

    def back_plane(i, _):
        p = first_own + i
        s3 = spre[pl.ds(pl.multiple_of(p * 3 * mband, 3 * mband), 9 * mband), :]
        c3 = scot[pl.ds(pl.multiple_of(p * 3 * mband, 3 * mband), 9 * mband), :]
        cg[i] = mul(b3_ref[:, : 9 * mband], s3) * (2.0 * inv)
        acc1[...] += mul_t(s3, cost[pl.ds(pl.multiple_of((p + 1) * band, band), band), :])
        acc2[:, :mband] += mul_t(c3, hid[pl.ds(pl.multiple_of(p * mband, mband), mband), :])
        return 0

    lax.fori_loop(0, own, back_plane, 0)

    def fold(acc, block, offset):
        rows = acc[...].reshape(9, height, mid, 128)
        lane = lax.broadcasted_iota(jnp.int32, (1, 1, 128), 2)
        total = None
        for g in range(height):
            ok = (lane >= (g - 1) * block) & (lane < (g + 2) * block) & (lane < height * block)
            part = jnp.where(ok, rows[:, g], 0.0).reshape(9 * mid, 128)
            turn = (offset - (g - 1) * block) % 128
            if turn:
                part = pltpu.roll(part, turn, 1)
            total = part if total is None else total + part
        return total

    ar[0] = fold(acc1, chans, 0) + fold(acc2, mid, 3 * chans)
    reduce_copies = []

    def reduce_begin():
        k = len(reduce_copies)
        if k < steps:
            reduce_copies.append(begin(remote(17 + k, ar.at[k], ar_in.at[k], partners[k])))

    def reduce_next():
        k = len(reduce_copies)
        if k <= steps and k > 0:
            reduce_copies[k - 1].wait_recv()
            ar[k] = ar[k - 1] + ar_in[k - 1]

    reduce_begin()

    def slot_back(t, emit):
        s = slot(t)
        weight = weight_of(s)

        def plane(i, _):
            p = first_own + i
            c, fy, left, right = weights(s, p)
            carried = None
            for h in range(height):
                rows = slice(h * chans, (h + 1) * chans)
                grad = (weight * cg[i, rows, :]) * (warp[t, p, rows, :] - mean[p, rows, :])
                taps[rows, :] = (left * grad + pltpu.roll(right * grad, 1, 1)).astype(taps.dtype)
            spread = turned(taps[...], -c)
            for h in range(height):
                rows = slice(h * chans, (h + 1) * chans)
                value = (1.0 - fy) * spread[rows]
                if carried is not None:
                    value = value + carried
                carried = fy * spread[rows]
                pad[i, rows, :] = value
            pad[i, height * chans :, :] = carried
            return 0

        lax.fori_loop(0, own, plane, 0)
        starts = [row_of(s, first_own + i) for i in range(own)]
        for r in range(held):
            total = None
            for i in range(own):
                part = jnp.zeros((chans, width), pad.dtype)
                for k in range(lead + 1):
                    if 0 <= r - k <= height:
                        row = pad[i, (r - k) * chans : (r - k + 1) * chans, :]
                        part = jnp.where(starts[i] == k, row, part)
                total = part if total is None else total + part
            for e in range(2):
                emit(e, slice(r * half, (r + 1) * half), total[e * half : (e + 1) * half])

    def to_mate(n):
        def emit(e, rows, value):
            a_send[n, e, rows, :] = value.astype(a_send.dtype)

        return emit

    def outward(n):
        def emit(e, rows, value):
            out_grad[n, e, rows, :] = value

        return emit

    slot_back(3, to_mate(1))
    a1 = begin(remote(8, a_send.at[1], a_recv.at[1], (mate, me)))
    reduce_next()
    reduce_begin()
    slot_back(0, outward(0))
    b_send[0] = out_grad[0, other].astype(b_send.dtype)
    b0 = begin(remote(9, b_send.at[0], b_recv.at[0], (cam, other)))
    reduce_next()
    reduce_begin()
    slot_back(1, outward(1))
    a1.wait_recv()
    b_send[1] = (out_grad[1, other] + a_recv[1, other].astype(jnp.float32)).astype(b_send.dtype)
    b1 = begin(remote(10, b_send.at[1], b_recv.at[1], (cam, other)))
    b0.wait_recv()
    c_send[0] = (out_grad[0, me] + b_recv[0].astype(jnp.float32)).astype(c_send.dtype)
    c0 = begin(remote(12, c_send.at[0], c_recv.at[0], (at(2), me)))
    reduce_next()
    reduce_begin()
    slot_back(2, to_mate(0))
    a0 = begin(remote(7, a_send.at[0], a_recv.at[0], (mate, me)))
    b1.wait_recv()
    c_send[1] = (
        out_grad[1, me] + a_recv[1, me].astype(jnp.float32) + b_recv[1].astype(jnp.float32)
    ).astype(c_send.dtype)
    c1 = begin(remote(13, c_send.at[1], c_recv.at[1], (at(1), me)))
    reduce_next()
    reduce_begin()

    for h in range(height):
        rows = slice(h * chans, (h + 1) * chans)
        ref = feat_ref[(top + h) * chans : (top + h + 1) * chans, :].astype(jnp.float32)
        total = None
        for i in range(own):
            term = cg[i, rows, :] * (ref - mean[first_own + i, rows, :])
            total = term if total is None else total + term
        for e in range(2):
            own_grad[e, (top + h) * half : (top + h + 1) * half, :] = total[e * half : (e + 1) * half]
    a0.wait_recv()
    b_send[2] = (own_grad[other] + a_recv[0, other].astype(jnp.float32)).astype(b_send.dtype)
    b2 = begin(remote(11, b_send.at[2], b_recv.at[2], (cam, other)))
    while len(reduce_copies) < steps:
        reduce_next()
        reduce_begin()
    reduce_next()
    wsum_ref[...] = ar[steps]
    b2.wait_recv()
    own_grad[me] = own_grad[me] + a_recv[0, me].astype(jnp.float32) + b_recv[2].astype(jnp.float32)
    c0.wait_recv()
    c1.wait_recv()
    grad_ref[...] = own_grad[me] + (c_recv[0].astype(jnp.float32) + c_recv[1].astype(jnp.float32))
    for copy in started:
        copy.wait_send()


def shards(
    features, view_mask, row_offset, frac_row, col_offset, frac_col,
    first_kernel, first_bias, second_kernel, cotangent,
):
    cams, slabs = lax.axis_size("cam"), lax.axis_size("depth")
    _, chans, held, width = features.shape
    mid = first_kernel.shape[0]
    _, _, own, height, _ = cotangent.shape
    band, mband, half = height * chans, height * mid, chans // 2
    assert slabs == 2 and 2 <= own <= 64 and band == 128 and width % 256 == 0 and cams & (cams - 1) == 0
    planes = own + 2
    steps = cams.bit_length()

    wide = ((0, 0), (0, 128 - own))
    ints = jnp.pad(jnp.concatenate([row_offset[0], col_offset[0]]), wide)
    floats = jnp.pad(jnp.concatenate([frac_row[0], frac_col[0]]), wide)
    order = (2, 3, 4, 0, 1)
    w1 = jnp.transpose(first_kernel, order)
    w2 = jnp.transpose(second_kernel, order)

    f32, bf16, i32 = jnp.float32, jnp.bfloat16, jnp.int32
    rows = held * half
    taps_rows = -(-9 * mband // 128) * 128
    grads, wsum = pl.pallas_call(
        functools.partial(compute, (chans, mid, height, held, width, own, planes, cams)),
        out_shape=(
            jax.ShapeDtypeStruct((rows, width), f32),
            jax.ShapeDtypeStruct((9 * mid, 128), f32),
        ),
        in_specs=[VMEM] * 4 + [SMEM] * 2 + [VMEM] * 2,
        out_specs=(VMEM, VMEM),
        scratch_shapes=[
            pltpu.VMEM((4, held * chans, width), bf16),
            pltpu.VMEM((2 * mband, width), bf16),
            pltpu.VMEM((8, 128), i32),
            pltpu.VMEM((8, 128), f32),
            pltpu.SMEM((2, 8, 128), i32),
            pltpu.SMEM((2, 8, 128), f32),
            pltpu.VMEM((4, planes, band, width), f32),
            pltpu.VMEM((planes, band, width), f32),
            pltpu.VMEM(((planes + 2) * band, width), bf16),
            pltpu.VMEM(((planes + 2) * 3 * mband, width), bf16),
            pltpu.VMEM(((planes + 2) * 3 * mband, width), bf16),
            pltpu.VMEM((planes * mband, width), bf16),
            pltpu.VMEM((9 * mband, 128), f32),
            pltpu.VMEM((9 * mband, 128), f32),
            pltpu.VMEM((own, band, width), f32),
            pltpu.VMEM((own, band + chans, width), f32),
            pltpu.VMEM((band, width), bf16),
            pltpu.VMEM((2, rows, width), f32),
            pltpu.VMEM((2, 2, rows, width), f32),
            pltpu.VMEM((2, 2, rows, width), bf16),
            pltpu.VMEM((2, 2, rows, width), bf16),
            pltpu.VMEM((3, rows, width), bf16),
            pltpu.VMEM((3, rows, width), bf16),
            pltpu.VMEM((2, rows, width), bf16),
            pltpu.VMEM((2, rows, width), bf16),
            pltpu.VMEM((steps + 1, 9 * mid, 128), f32),
            pltpu.VMEM((steps, 9 * mid, 128), f32),
            pltpu.VMEM((chans, held, width), f32),
            pltpu.VMEM((mid, own * height, width), f32),
            pltpu.VMEM((held * chans, width), bf16),
            pltpu.VMEM((own * mband, width), bf16),
            pltpu.VMEM((3 * mband, 3 * band), bf16),
            pltpu.VMEM((3 * mband, 3 * band), f32),
            pltpu.VMEM((mband, taps_rows), bf16),
            pltpu.VMEM((taps_rows, 128), f32),
            pltpu.VMEM((band, taps_rows), bf16),
            pltpu.VMEM((taps_rows, 128), f32),
            pltpu.VMEM((mband, width), f32),
            pltpu.SemaphoreType.DMA((17 + steps,)),
            pltpu.SemaphoreType.DMA((17 + steps,)),
            pltpu.SemaphoreType.DMA((4,)),
        ],
        compiler_params=pltpu.CompilerParams(
            vmem_limit_bytes=48 * 2**20, collective_id=0, has_side_effects=True
        ),
        name="core",
    )(features[0], cotangent[0], ints, floats, view_mask[0], first_bias, w1, w2)

    feature_grad = jnp.transpose(grads.reshape(held, half, width), (1, 0, 2))
    scale = (cams * slabs * own * height * width) ** (-0.5)
    taps = (wsum * scale).reshape(3, 3, mid, 128)[::-1, ::-1]
    first = taps[..., : 3 * chans].reshape(3, 3, mid, 3, chans)
    second = taps[..., 3 * chans : 3 * chans + 3 * mid].reshape(3, 3, mid, 3, mid)
    order = (2, 4, 0, 3, 1)
    return feature_grad[None], jnp.transpose(first, order), jnp.transpose(second, order)


def solution(mesh):
    placed = (
        P("cam", None, None, None),
        P("cam", None),
        P("cam", None, "depth"),
        P("cam", None, "depth"),
        P("cam", None, "depth"),
        P("cam", None, "depth"),
        P(),
        P(),
        P(),
        P("cam", None, "depth", None, None),
    )
    return jax.shard_map(
        shards,
        mesh=mesh,
        in_specs=placed,
        out_specs=(P("cam", "depth", None, None), P(), P()),
        check_vma=False,
    )
```

```python
import functools

import jax
import jax.numpy as jnp
from jax import lax
from jax.experimental import pallas as pl
from jax.experimental.pallas import tpu as pltpu
from jax.sharding import PartitionSpec as P

view_offsets = (-2, -1, 1, 2)
MESH = pl.DeviceIdType.MESH
HBM = pl.BlockSpec(memory_space=pltpu.HBM)
VMEM = pl.BlockSpec(memory_space=pltpu.VMEM)


def mul(a, b):
    return jnp.dot(a, b, preferred_element_type=jnp.float32)


def mul_t(a, b):
    return lax.dot_general(a, b, (((1,), (1,)), ((), ())), preferred_element_type=jnp.float32)


def lanes(width):
    return lax.broadcasted_iota(jnp.int32, (1, width), 1)


def from_left(x):
    width = x.shape[1]
    return jnp.where(lanes(width) > 0, pltpu.roll(x, 1, 1), 0.0)


def from_right(x):
    width = x.shape[1]
    return jnp.where(lanes(width) < width - 1, pltpu.roll(x, width - 1, 1), 0.0)


def turned(x, by):
    count, width = x.shape
    parts = []
    for start in range(0, width, 256):
        before = (start - 128) % width
        after = (start + 256) % width
        parts.append(
            jnp.concatenate(
                [x[:, before : before + 128], x[:, start : start + 256], x[:, after : after + 128]], axis=1
            )
        )
    apart = lax.broadcasted_iota(jnp.int32, (128, 128), 0) - lax.broadcasted_iota(jnp.int32, (128, 128), 1)
    low, mid, high = (jnp.where(apart == by - d, 1.0, 0.0).astype(x.dtype) for d in (-128, 0, 128))
    none = jnp.zeros_like(mid)
    pick = jnp.concatenate(
        [jnp.concatenate([low, mid, high, none], axis=0), jnp.concatenate([none, low, mid, high], axis=0)], axis=1
    )
    out = mul(jnp.concatenate(parts, axis=0), pick)
    return jnp.concatenate([out[i * count : (i + 1) * count] for i in range(width // 256)], axis=1)


def in_steps(count, size, body):
    if count % size:
        size = 1

    def step(i, _):
        for n in range(size):
            body(i * size + n, 0)
        return 0

    if count == size:
        step(0, 0)
    else:
        lax.fori_loop(0, count // size, step, 0)


def compute(
    dims,
    raw_hbm, cotangent_hbm, row_hbm, col_hbm, fy_hbm, fx_hbm, mask_hbm, bias_hbm, w1_hbm, w2_hbm,
    grad_ref, wsum_ref,
    raw_ref, cotangent_ref, mask_ref, bias_ref, w1_ref, w2_ref,
    bands, halo, ints_in, floats_in, ints, floats,
    warp, mean, cost, scot, spre, hid, acc1, acc2, cg, pad, taps,
    own_grad, out_grad, a_send, a_recv, b_send, b_recv, c_send, c_recv, ar, ar_in,
    wide, cot_wide, feat_ref, cot_ref, b1_ref, b1_wide, b2_ref, b2_wide, b3_ref, b3_wide, bias,
    send_sem, recv_sem, local_sem,
):
    chans, mid, height, held, width, own, planes, cams = dims
    top = (held - height) // 2
    lead = held - height - 1
    half = chans // 2
    band = height * chans
    mband = height * mid
    steps = ar_in.shape[0]

    cam = lax.axis_index("cam")
    me = lax.axis_index("depth")
    other = 1 - me
    first_own = (planes - own) * me
    odd = lax.rem(cam, 2)

    def at(offset):
        return lax.rem(cam + cams + offset * (2 * odd - 1), cams)

    def slot(t):
        return t + odd * (3 - 2 * t)

    mate = at(-1)
    partners = []
    reach = 1
    while reach < cams:
        bit = lax.rem(cam // reach, 2)
        partners.append((cam + reach * (1 - 2 * bit), me))
        reach *= 2
    partners.append((cam, other))

    fetches = [
        pltpu.make_async_copy(src, dst, local_sem.at[n])
        for n, (src, dst) in enumerate(
            [
                (raw_hbm, raw_ref), (cotangent_hbm, cotangent_ref), (w1_hbm, w1_ref), (w2_hbm, w2_ref),
                (row_hbm, ints.at[me, 0]), (col_hbm, ints.at[me, 1]),
                (fy_hbm, floats.at[me, 0]), (fx_hbm, floats.at[me, 1]),
                (mask_hbm, mask_ref), (bias_hbm, bias_ref),
            ]
        )
    ]
    for fetch in fetches:
        fetch.start()

    barrier = pltpu.get_barrier_semaphore()
    greeted = [(at(-2), me), (at(-1), me), (at(1), me), (at(2), me)] + partners
    for device in greeted:
        pl.semaphore_signal(barrier, inc=1, device_id=device, device_id_type=MESH)

    fetches[0].wait()
    wide[...] = raw_ref[...].astype(jnp.float32)
    for r in range(held):
        feat_ref[r * chans : (r + 1) * chans, :] = wide[:, r, :].astype(feat_ref.dtype)

    pl.semaphore_wait(barrier, len(greeted))

    started = []

    def remote(n, src, dst, device):
        return pltpu.make_async_remote_copy(
            src_ref=src, dst_ref=dst, send_sem=send_sem.at[n], recv_sem=recv_sem.at[n],
            device_id=device, device_id_type=MESH,
        )

    def begin(copy):
        copy.start()
        started.append(copy)
        return copy

    span = held // 2 * chans

    def part(ref, e):
        return ref.at[pl.ds(pl.multiple_of(e * span, span), span), :]

    feat1 = begin(remote(4, part(feat_ref, me), part(bands.at[1], me), (at(1), me)))
    feat0 = begin(remote(3, part(feat_ref, me), part(bands.at[0], me), (at(-2), me)))
    feat2 = begin(remote(5, feat_ref, bands.at[2], (mate, me)))
    scalar_copies = [
        begin(remote(n, src, dst, (cam, other)))
        for n, src, dst in (
            (0, row_hbm, ints_in.at[0]), (1, col_hbm, ints_in.at[1]),
            (17, fy_hbm, floats_in.at[0]), (18, fx_hbm, floats_in.at[1]),
        )
    ]

    fetches[1].wait()
    for i in range(own):
        cot_wide[:, i * height : (i + 1) * height, :] = cotangent_ref[:, i].astype(jnp.float32)
    for i in range(own):
        cot_ref[i * mband : (i + 1) * mband, :] = jnp.concatenate(
            [cot_wide[:, i * height + h, :] for h in range(height)], axis=0
        ).astype(cot_ref.dtype)
    edge = pl.multiple_of((own - 2) * other * mband, mband)
    halo_copy = begin(remote(2, cot_ref.at[pl.ds(edge, 2 * mband), :], halo, (cam, other)))

    for end in (0, planes + 1):
        scot[end * 3 * mband : (end + 1) * 3 * mband, :] = jnp.zeros((3 * mband, width), scot.dtype)
        spre[end * 3 * mband : (end + 1) * 3 * mband, :] = jnp.zeros((3 * mband, width), spre.dtype)
        cost[end * band : (end + 1) * band, :] = jnp.zeros((band, width), cost.dtype)

    def shift_plane(plane, p):
        wide = plane.astype(jnp.float32)
        base = pl.multiple_of((p + 1) * 3 * mband, mband)
        scot[pl.ds(base, mband), :] = from_left(wide).astype(scot.dtype)
        scot[pl.ds(base + mband, mband), :] = plane
        scot[pl.ds(base + 2 * mband, mband), :] = from_right(wide).astype(scot.dtype)

    for i in range(own):
        shift_plane(cot_ref[i * mband : (i + 1) * mband, :], first_own + i)

    def blocks(w_ref, block, kd, kw):
        taps = []
        for kh in range(3):
            tap = w_ref[kd, kh, kw].astype(jnp.float32)
            taps.append(jnp.concatenate([tap, jnp.zeros((mid, 128 - block), jnp.float32)], axis=1))
        found = []
        for h in range(height):
            total = None
            for kh in range(3):
                to = h + kh - 1
                if 0 <= to < height:
                    moved = taps[kh] if to == 0 else pltpu.roll(taps[kh], to * block, 1)
                    total = moved if total is None else total + moved
            found.append(total)
        return found

    for fetch in fetches[2:]:
        fetch.wait()
    for kd in range(3):
        for kw in range(3):
            for h, value in enumerate(blocks(w1_ref, chans, kd, kw)):
                row = (kw * height + h) * mid
                b1_wide[row : row + mid, kd * 128 : (kd + 1) * 128] = value
                row = (((2 - kd) * 3 + 2 - kw) * height + h) * mid
                b3_wide[row : row + mid, :] = value
            for h, value in enumerate(blocks(w2_ref, mid, kd, kw)):
                row = (((2 - kd) * 3 + 2 - kw) * height + h) * mid
                b2_wide[row : row + mid, :] = value
    for ref in (b2_wide, b3_wide):
        ref[9 * mband :, :] = jnp.zeros((ref.shape[0] - 9 * mband, 128), jnp.float32)
    b1_ref[...] = b1_wide[...].astype(b1_ref.dtype)
    b2_ref[...] = jnp.transpose(b2_wide[...])[:mband].astype(b2_ref.dtype)
    b3_ref[...] = jnp.transpose(b3_wide[...]).astype(b3_ref.dtype)
    which = lax.rem(lax.broadcasted_iota(jnp.int32, (mband, width), 0), mid)
    column = jnp.zeros((mband, width), jnp.float32)
    for o in range(mid):
        column = jnp.where(which == o, bias_ref[0, o], column)
    bias[...] = column

    def weight_of(s):
        return mask_ref[0, s].astype(jnp.float32)

    count = 1.0 + weight_of(0) + weight_of(1) + weight_of(2) + weight_of(3)
    inv = 1.0 / jnp.full((1, width), count, jnp.float32)

    arrivals = []
    for n, (src, dst) in enumerate(
        [(ints_in, ints), (ints_in, ints), (floats_in, floats), (floats_in, floats)]
    ):
        scalar_copies[n].wait_recv()
        arrivals.append(pltpu.make_async_copy(src.at[n % 2], dst.at[other, n % 2], local_sem.at[10 + n]))
        arrivals[-1].start()
    halo_copy.wait_recv()
    for i in range(2):
        shift_plane(halo[i * mband : (i + 1) * mband, :], own * other + i)
    for arrival in arrivals:
        arrival.wait()

    def place(p):
        at_plane = p + me * (2 * own - planes)
        return at_plane // own, lax.rem(at_plane, own)

    def row_of(s, p):
        slab, lane = place(p)
        return ints[slab, 0, s, lane]

    def weights(s, p):
        slab, lane = place(p)
        c = ints[slab, 1, s, lane]
        fy = floats[slab, 0, s, lane]
        fx = floats[slab, 1, s, lane]
        spot = lanes(width) + c
        left = jnp.where((spot >= 0) & (spot < width), 1.0 - fx, 0.0)
        right = jnp.where((spot >= -1) & (spot < width - 1), fx, 0.0)
        return c, fy, left, right

    def warp_slot(t, last):
        s = slot(t)

        def plane(p, _):
            c, fy, left, right = weights(s, p)
            r = row_of(s, p)
            window = bands[t, : band + chans, :]
            for k in range(1, lead + 1):
                window = jnp.where(r == k, bands[t, k * chans : band + (k + 1) * chans, :], window)
            here = turned(window, c)
            for h in range(height):
                rows = slice(h * chans, (h + 1) * chans)
                mixed = (1.0 - fy) * here[rows] + fy * here[(h + 1) * chans : (h + 2) * chans]
                warped = left * mixed + right * pltpu.roll(mixed, width - 1, 1)
                warp[t, p, rows, :] = warped
                if last:
                    ref = feat_ref[(top + h) * chans : (top + h + 1) * chans, :].astype(jnp.float32)
                    first = ref
                    second = ref * ref
                    for u in range(4):
                        view = warped if u == t else warp[u, p, rows, :]
                        weighted = weight_of(slot(u)) * view
                        first = first + weighted
                        second = second + weighted * view
                    average = first * inv
                    mean[p, rows, :] = average
                    spot = pl.multiple_of((p + 1) * band + h * chans, chans)
                    cost[pl.ds(spot, chans), :] = (second * inv - average * average).astype(cost.dtype)
            return 0

        in_steps(planes, 2, plane)

    feat2.wait_recv()
    warp_slot(2, False)
    feat1.wait_recv()
    over1 = begin(remote(14, part(bands.at[1], me), part(bands.at[1], me), (cam, other)))
    feat3 = begin(remote(6, part(bands.at[1], me), part(bands.at[3], me), (mate, me)))
    feat0.wait_recv()
    over0 = begin(remote(15, part(bands.at[0], me), part(bands.at[0], me), (cam, other)))
    over1.wait_recv()
    over3 = begin(remote(16, part(bands.at[1], other), part(bands.at[3], other), (mate, me)))
    warp_slot(1, False)
    feat3.wait_recv()
    over3.wait_recv()
    warp_slot(3, False)
    over0.wait_recv()
    warp_slot(0, True)

    def middle(i, _):
        p = first_own // 2 + i
        x = cost[pl.ds(pl.multiple_of(p * band, band), 3 * band), :]
        parts = mul(b1_ref[...], x)
        pre = from_left(parts[:mband]) + parts[mband : 2 * mband] + from_right(parts[2 * mband :])
        pre = pre + bias[...]
        gate = jax.nn.sigmoid(pre)
        hid[pl.ds(pl.multiple_of(p * mband, mband), mband), :] = (pre * gate).astype(hid.dtype)
        y = scot[pl.ds(pl.multiple_of(p * 3 * mband, 3 * mband), 3 * 3 * mband), :]
        back = mul(b2_ref[:, : 9 * mband], y) * (gate * (1.0 + pre * (1.0 - gate)))
        base = pl.multiple_of((p + 1) * 3 * mband, mband)
        spre[pl.ds(base, mband), :] = from_left(back).astype(spre.dtype)
        spre[pl.ds(base + mband, mband), :] = back.astype(spre.dtype)
        spre[pl.ds(base + 2 * mband, mband), :] = from_right(back).astype(spre.dtype)
        return 0

    in_steps(own + (planes - own) // 2, own + (planes - own) // 2, middle)

    acc1[...] = jnp.zeros_like(acc1)
    acc2[...] = jnp.zeros_like(acc2)
    own_grad[...] = jnp.zeros_like(own_grad)

    def back_plane(i, _):
        p = first_own + i
        s3 = spre[pl.ds(pl.multiple_of(p * 3 * mband, 3 * mband), 9 * mband), :]
        c3 = scot[pl.ds(pl.multiple_of(p * 3 * mband, 3 * mband), 9 * mband), :]
        cg[i] = mul(b3_ref[:, : 9 * mband], s3) * (2.0 * inv)
        acc1[...] += mul_t(s3, cost[pl.ds(pl.multiple_of((p + 1) * band, band), band), :])
        acc2[:, :mband] += mul_t(c3, hid[pl.ds(pl.multiple_of(p * mband, mband), mband), :])
        return 0

    in_steps(own, 2, back_plane)

    def fold(acc, block, offset):
        rows = acc[...].reshape(9, height, mid, 128)
        lane = lax.broadcasted_iota(jnp.int32, (1, 1, 128), 2)
        total = None
        for g in range(height):
            ok = (lane >= (g - 1) * block) & (lane < (g + 2) * block) & (lane < height * block)
            part = jnp.where(ok, rows[:, g], 0.0).reshape(9 * mid, 128)
            turn = (offset - (g - 1) * block) % 128
            if turn:
                part = pltpu.roll(part, turn, 1)
            total = part if total is None else total + part
        return total

    ar[0] = fold(acc1, chans, 0) + fold(acc2, mid, 3 * chans)
    reduce_copies = []

    def reduce_begin():
        k = len(reduce_copies)
        if k < steps:
            reduce_copies.append(begin(remote(19 + k, ar.at[k], ar_in.at[k], partners[k])))

    def reduce_next():
        k = len(reduce_copies)
        if k <= steps and k > 0:
            reduce_copies[k - 1].wait_recv()
            ar[k] = ar[k - 1] + ar_in[k - 1]

    reduce_begin()

    def slot_back(t, emit):
        s = slot(t)
        weight = weight_of(s)

        def plane(i, _):
            p = first_own + i
            c, fy, left, right = weights(s, p)
            carried = None
            for h in range(height):
                rows = slice(h * chans, (h + 1) * chans)
                grad = (weight * cg[i, rows, :]) * (warp[t, p, rows, :] - mean[p, rows, :])
                taps[rows, :] = (left * grad + pltpu.roll(right * grad, 1, 1)).astype(taps.dtype)
            spread = turned(taps[...], -c)
            for h in range(height):
                rows = slice(h * chans, (h + 1) * chans)
                value = (1.0 - fy) * spread[rows]
                if carried is not None:
                    value = value + carried
                carried = fy * spread[rows]
                pad[i, rows, :] = value
            pad[i, height * chans :, :] = carried
            return 0

        in_steps(own, 2, plane)
        starts = [row_of(s, first_own + i) for i in range(own)]
        for r in range(held):
            total = None
            for i in range(own):
                part = jnp.zeros((chans, width), pad.dtype)
                for k in range(lead + 1):
                    if 0 <= r - k <= height:
                        row = pad[i, (r - k) * chans : (r - k + 1) * chans, :]
                        part = jnp.where(starts[i] == k, row, part)
                total = part if total is None else total + part
            for e in range(2):
                emit(e, slice(r * half, (r + 1) * half), total[e * half : (e + 1) * half])

    def to_mate(n):
        def emit(e, rows, value):
            a_send[n, e, rows, :] = value.astype(a_send.dtype)

        return emit

    def outward(n):
        def emit(e, rows, value):
            out_grad[n, e, rows, :] = value

        return emit

    slot_back(3, to_mate(1))
    a1 = begin(remote(8, a_send.at[1], a_recv.at[1], (mate, me)))
    reduce_next()
    reduce_begin()
    slot_back(0, outward(0))
    b_send[0] = out_grad[0, other].astype(b_send.dtype)
    b0 = begin(remote(9, b_send.at[0], b_recv.at[0], (cam, other)))
    reduce_next()
    reduce_begin()
    slot_back(1, outward(1))
    a1.wait_recv()
    b_send[1] = (out_grad[1, other] + a_recv[1, other].astype(jnp.float32)).astype(b_send.dtype)
    b1 = begin(remote(10, b_send.at[1], b_recv.at[1], (cam, other)))
    b0.wait_recv()
    c_send[0] = (out_grad[0, me] + b_recv[0].astype(jnp.float32)).astype(c_send.dtype)
    c0 = begin(remote(12, c_send.at[0], c_recv.at[0], (at(2), me)))
    reduce_next()
    reduce_begin()
    slot_back(2, to_mate(0))
    a0 = begin(remote(7, a_send.at[0], a_recv.at[0], (mate, me)))
    b1.wait_recv()
    c_send[1] = (
        out_grad[1, me] + a_recv[1, me].astype(jnp.float32) + b_recv[1].astype(jnp.float32)
    ).astype(c_send.dtype)
    c1 = begin(remote(13, c_send.at[1], c_recv.at[1], (at(1), me)))
    reduce_next()
    reduce_begin()

    for h in range(height):
        rows = slice(h * chans, (h + 1) * chans)
        ref = feat_ref[(top + h) * chans : (top + h + 1) * chans, :].astype(jnp.float32)
        total = None
        for i in range(own):
            term = cg[i, rows, :] * (ref - mean[first_own + i, rows, :])
            total = term if total is None else total + term
        for e in range(2):
            own_grad[e, (top + h) * half : (top + h + 1) * half, :] = total[e * half : (e + 1) * half]
    a0.wait_recv()
    b_send[2] = (own_grad[other] + a_recv[0, other].astype(jnp.float32)).astype(b_send.dtype)
    b2 = begin(remote(11, b_send.at[2], b_recv.at[2], (cam, other)))
    while len(reduce_copies) < steps:
        reduce_next()
        reduce_begin()
    reduce_next()
    wsum_ref[...] = ar[steps]
    b2.wait_recv()
    own_grad[me] = own_grad[me] + a_recv[0, me].astype(jnp.float32) + b_recv[2].astype(jnp.float32)
    c0.wait_recv()
    c1.wait_recv()
    grad_ref[...] = own_grad[me] + (c_recv[0].astype(jnp.float32) + c_recv[1].astype(jnp.float32))
    for copy in started:
        copy.wait_send()


def shards(
    features, view_mask, row_offset, frac_row, col_offset, frac_col,
    first_kernel, first_bias, second_kernel, cotangent,
):
    cams, slabs = lax.axis_size("cam"), lax.axis_size("depth")
    _, chans, held, width = features.shape
    mid = first_kernel.shape[0]
    _, _, own, height, _ = cotangent.shape
    band, mband, half = height * chans, height * mid, chans // 2
    assert slabs == 2 and 2 <= own <= 64 and band == 128 and width % 256 == 0 and cams & (cams - 1) == 0
    planes = own + 2
    steps = cams.bit_length()

    order = (2, 3, 4, 0, 1)
    w1 = jnp.transpose(first_kernel, order)
    w2 = jnp.transpose(second_kernel, order)

    f32, bf16, i32 = jnp.float32, jnp.bfloat16, jnp.int32
    rows = held * half
    taps_rows = -(-9 * mband // 128) * 128
    grads, wsum = pl.pallas_call(
        functools.partial(compute, (chans, mid, height, held, width, own, planes, cams)),
        out_shape=(
            jax.ShapeDtypeStruct((rows, width), f32),
            jax.ShapeDtypeStruct((9 * mid, 128), f32),
        ),
        in_specs=[HBM] * 10,
        out_specs=(VMEM, VMEM),
        scratch_shapes=[
            pltpu.VMEM(features.shape[1:], bf16),
            pltpu.VMEM(cotangent.shape[1:], bf16),
            pltpu.SMEM((1, 4), i32),
            pltpu.SMEM((1, mid), f32),
            pltpu.VMEM(w1.shape, bf16),
            pltpu.VMEM(w2.shape, bf16),
            pltpu.VMEM((4, held * chans, width), bf16),
            pltpu.VMEM((2 * mband, width), bf16),
            pltpu.VMEM((2, 4, own), i32),
            pltpu.VMEM((2, 4, own), f32),
            pltpu.SMEM((2, 2, 4, own), i32),
            pltpu.SMEM((2, 2, 4, own), f32),
            pltpu.VMEM((4, planes, band, width), f32),
            pltpu.VMEM((planes, band, width), f32),
            pltpu.VMEM(((planes + 2) * band, width), bf16),
            pltpu.VMEM(((planes + 2) * 3 * mband, width), bf16),
            pltpu.VMEM(((planes + 2) * 3 * mband, width), bf16),
            pltpu.VMEM((planes * mband, width), bf16),
            pltpu.VMEM((9 * mband, 128), f32),
            pltpu.VMEM((9 * mband, 128), f32),
            pltpu.VMEM((own, band, width), f32),
            pltpu.VMEM((own, band + chans, width), f32),
            pltpu.VMEM((band, width), bf16),
            pltpu.VMEM((2, rows, width), f32),
            pltpu.VMEM((2, 2, rows, width), f32),
            pltpu.VMEM((2, 2, rows, width), bf16),
            pltpu.VMEM((2, 2, rows, width), bf16),
            pltpu.VMEM((3, rows, width), bf16),
            pltpu.VMEM((3, rows, width), bf16),
            pltpu.VMEM((2, rows, width), bf16),
            pltpu.VMEM((2, rows, width), bf16),
            pltpu.VMEM((steps + 1, 9 * mid, 128), f32),
            pltpu.VMEM((steps, 9 * mid, 128), f32),
            pltpu.VMEM((chans, held, width), f32),
            pltpu.VMEM((mid, own * height, width), f32),
            pltpu.VMEM((held * chans, width), bf16),
            pltpu.VMEM((own * mband, width), bf16),
            pltpu.VMEM((3 * mband, 3 * band), bf16),
            pltpu.VMEM((3 * mband, 3 * band), f32),
            pltpu.VMEM((mband, taps_rows), bf16),
            pltpu.VMEM((taps_rows, 128), f32),
            pltpu.VMEM((band, taps_rows), bf16),
            pltpu.VMEM((taps_rows, 128), f32),
            pltpu.VMEM((mband, width), f32),
            pltpu.SemaphoreType.DMA((19 + steps,)),
            pltpu.SemaphoreType.DMA((19 + steps,)),
            pltpu.SemaphoreType.DMA((14,)),
        ],
        compiler_params=pltpu.CompilerParams(
            vmem_limit_bytes=48 * 2**20, collective_id=0, has_side_effects=True
        ),
        name="core",
    )(
        features[0], cotangent[0], row_offset[0], col_offset[0], frac_row[0], frac_col[0],
        view_mask, first_bias[None], w1, w2,
    )

    feature_grad = jnp.transpose(grads.reshape(held, half, width), (1, 0, 2))
    scale = (cams * slabs * own * height * width) ** (-0.5)
    taps = (wsum * scale).reshape(3, 3, mid, 128)[::-1, ::-1]
    first = taps[..., : 3 * chans].reshape(3, 3, mid, 3, chans)
    second = taps[..., 3 * chans : 3 * chans + 3 * mid].reshape(3, 3, mid, 3, mid)
    order = (2, 4, 0, 3, 1)
    return feature_grad[None], jnp.transpose(first, order), jnp.transpose(second, order)


def solution(mesh):
    placed = (
        P("cam", None, None, None),
        P("cam", None),
        P("cam", None, "depth"),
        P("cam", None, "depth"),
        P("cam", None, "depth"),
        P("cam", None, "depth"),
        P(),
        P(),
        P(),
        P("cam", None, "depth", None, None),
    )
    return jax.shard_map(
        shards,
        mesh=mesh,
        in_specs=placed,
        out_specs=(P("cam", "depth", None, None), P(), P()),
        check_vma=False,
    )
```

```python
import functools

import jax
import jax.numpy as jnp
from jax import lax
from jax.experimental import pallas as pl
from jax.experimental.pallas import tpu as pltpu
from jax.sharding import PartitionSpec as P

view_offsets = (-2, -1, 1, 2)
MESH = pl.DeviceIdType.MESH
HBM = pl.BlockSpec(memory_space=pltpu.HBM)
VMEM = pl.BlockSpec(memory_space=pltpu.VMEM)


def mul(a, b):
    return jnp.dot(a, b, preferred_element_type=jnp.float32)


def mul_t(a, b):
    return lax.dot_general(a, b, (((1,), (1,)), ((), ())), preferred_element_type=jnp.float32)


def lanes(width):
    return lax.broadcasted_iota(jnp.int32, (1, width), 1)


def from_left(x):
    width = x.shape[1]
    return jnp.where(lanes(width) > 0, pltpu.roll(x, 1, 1), 0.0)


def from_right(x):
    width = x.shape[1]
    return jnp.where(lanes(width) < width - 1, pltpu.roll(x, width - 1, 1), 0.0)


def turned(x, by):
    count, width = x.shape
    parts = []
    for start in range(0, width, 256):
        before = (start - 128) % width
        after = (start + 256) % width
        parts.append(
            jnp.concatenate(
                [x[:, before : before + 128], x[:, start : start + 256], x[:, after : after + 128]], axis=1
            )
        )
    apart = lax.broadcasted_iota(jnp.int32, (128, 128), 0) - lax.broadcasted_iota(jnp.int32, (128, 128), 1)
    low, mid, high = (jnp.where(apart == by - d, 1.0, 0.0).astype(x.dtype) for d in (-128, 0, 128))
    none = jnp.zeros_like(mid)
    pick = jnp.concatenate(
        [jnp.concatenate([low, mid, high, none], axis=0), jnp.concatenate([none, low, mid, high], axis=0)], axis=1
    )
    out = mul(jnp.concatenate(parts, axis=0), pick)
    return jnp.concatenate([out[i * count : (i + 1) * count] for i in range(width // 256)], axis=1)


def in_steps(count, size, body):
    if count % size:
        size = 1

    def step(i, _):
        for n in range(size):
            body(i * size + n, 0)
        return 0

    if count == size:
        step(0, 0)
    else:
        lax.fori_loop(0, count // size, step, 0)


def compute(
    dims,
    raw_hbm, cotangent_hbm, row_hbm, col_hbm, fy_hbm, fx_hbm, mask_hbm, bias_hbm, w1_hbm, w2_hbm,
    grad_ref, wsum_ref,
    raw_ref, cotangent_ref, mask_ref, bias_ref, w1_ref, w2_ref,
    bands, halo, ints_in, floats_in, ints, floats,
    warp, mean, cost, scot, spre, hid, acc1, acc2, cg, pad, taps,
    own_grad, out_grad, a_send, a_recv, b_send, b_recv, c_send, c_recv, ar, ar_in,
    wide, cot_wide, feat_ref, cot_ref, b1_ref, b1_wide, b2_ref, b2_wide, b3_ref, b3_wide, bias,
    send_sem, recv_sem, local_sem,
):
    chans, mid, height, held, width, own, planes, cams = dims
    top = (held - height) // 2
    lead = held - height - 1
    half = chans // 2
    band = height * chans
    mband = height * mid
    steps = ar_in.shape[0]

    cam = lax.axis_index("cam")
    me = lax.axis_index("depth")
    other = 1 - me
    first_own = (planes - own) * me
    odd = lax.rem(cam, 2)

    def at(offset):
        return lax.rem(cam + cams + offset * (2 * odd - 1), cams)

    def slot(t):
        return t + odd * (3 - 2 * t)

    mate = at(-1)
    partners = []
    reach = 1
    while reach < cams:
        bit = lax.rem(cam // reach, 2)
        partners.append((cam + reach * (1 - 2 * bit), me))
        reach *= 2
    partners.append((cam, other))

    fetches = [
        pltpu.make_async_copy(src, dst, local_sem.at[n])
        for n, (src, dst) in enumerate(
            [
                (raw_hbm, raw_ref), (cotangent_hbm, cotangent_ref), (w1_hbm, w1_ref), (w2_hbm, w2_ref),
                (row_hbm, ints.at[me, 0]), (col_hbm, ints.at[me, 1]),
                (fy_hbm, floats.at[me, 0]), (fx_hbm, floats.at[me, 1]),
                (mask_hbm, mask_ref), (bias_hbm, bias_ref),
            ]
        )
    ]
    for fetch in fetches:
        fetch.start()

    barrier = pltpu.get_barrier_semaphore()
    greeted = [(at(-2), me), (at(-1), me), (at(1), me), (at(2), me)] + partners
    for device in greeted:
        pl.semaphore_signal(barrier, inc=1, device_id=device, device_id_type=MESH)

    fetches[0].wait()
    wide[...] = raw_ref[...].astype(jnp.float32)
    for r in range(held):
        feat_ref[r * chans : (r + 1) * chans, :] = wide[:, r, :].astype(feat_ref.dtype)

    pl.semaphore_wait(barrier, len(greeted))

    started = []

    def remote(n, src, dst, device):
        return pltpu.make_async_remote_copy(
            src_ref=src, dst_ref=dst, send_sem=send_sem.at[n], recv_sem=recv_sem.at[n],
            device_id=device, device_id_type=MESH,
        )

    def begin(copy):
        copy.start()
        started.append(copy)
        return copy

    span = held // 2 * chans

    def part(ref, e):
        return ref.at[pl.ds(pl.multiple_of(e * span, span), span), :]

    feat1 = begin(remote(4, part(feat_ref, me), part(bands.at[1], me), (at(1), me)))
    feat0 = begin(remote(3, part(feat_ref, me), part(bands.at[0], me), (at(-2), me)))
    feat2 = begin(remote(5, feat_ref, bands.at[2], (mate, me)))
    scalar_copies = [
        begin(remote(n, src, dst, (cam, other)))
        for n, src, dst in (
            (0, row_hbm, ints_in.at[0]), (1, col_hbm, ints_in.at[1]),
            (17, fy_hbm, floats_in.at[0]), (18, fx_hbm, floats_in.at[1]),
        )
    ]

    fetches[1].wait()
    for i in range(own):
        cot_wide[:, i * height : (i + 1) * height, :] = cotangent_ref[:, i].astype(jnp.float32)
    for i in range(own):
        cot_ref[i * mband : (i + 1) * mband, :] = jnp.concatenate(
            [cot_wide[:, i * height + h, :] for h in range(height)], axis=0
        ).astype(cot_ref.dtype)
    edge = pl.multiple_of((own - 2) * other * mband, mband)
    halo_copy = begin(remote(2, cot_ref.at[pl.ds(edge, 2 * mband), :], halo, (cam, other)))

    for end in (0, planes + 1):
        scot[end * 3 * mband : (end + 1) * 3 * mband, :] = jnp.zeros((3 * mband, width), scot.dtype)
        spre[end * 3 * mband : (end + 1) * 3 * mband, :] = jnp.zeros((3 * mband, width), spre.dtype)
        cost[end * band : (end + 1) * band, :] = jnp.zeros((band, width), cost.dtype)

    def shift_plane(plane, p):
        wide = plane.astype(jnp.float32)
        base = pl.multiple_of((p + 1) * 3 * mband, mband)
        scot[pl.ds(base, mband), :] = from_left(wide).astype(scot.dtype)
        scot[pl.ds(base + mband, mband), :] = plane
        scot[pl.ds(base + 2 * mband, mband), :] = from_right(wide).astype(scot.dtype)

    for i in range(own):
        shift_plane(cot_ref[i * mband : (i + 1) * mband, :], first_own + i)

    def blocks(w_ref, block, kd, kw):
        taps = []
        for kh in range(3):
            tap = w_ref[kd, kh, kw].astype(jnp.float32)
            taps.append(jnp.concatenate([tap, jnp.zeros((mid, 128 - block), jnp.float32)], axis=1))
        found = []
        for h in range(height):
            total = None
            for kh in range(3):
                to = h + kh - 1
                if 0 <= to < height:
                    moved = taps[kh] if to == 0 else pltpu.roll(taps[kh], to * block, 1)
                    total = moved if total is None else total + moved
            found.append(total)
        return found

    for fetch in fetches[2:]:
        fetch.wait()
    for kd in range(3):
        for kw in range(3):
            for h, value in enumerate(blocks(w1_ref, chans, kd, kw)):
                row = (kw * height + h) * mid
                b1_wide[row : row + mid, kd * 128 : (kd + 1) * 128] = value
                row = (((2 - kd) * 3 + 2 - kw) * height + h) * mid
                b3_wide[row : row + mid, :] = value
            for h, value in enumerate(blocks(w2_ref, mid, kd, kw)):
                row = (((2 - kd) * 3 + 2 - kw) * height + h) * mid
                b2_wide[row : row + mid, :] = value
    for ref in (b2_wide, b3_wide):
        ref[9 * mband :, :] = jnp.zeros((ref.shape[0] - 9 * mband, 128), jnp.float32)
    b1_ref[...] = b1_wide[...].astype(b1_ref.dtype)
    b2_ref[...] = jnp.transpose(b2_wide[...])[:mband].astype(b2_ref.dtype)
    b3_ref[...] = jnp.transpose(b3_wide[...]).astype(b3_ref.dtype)
    which = lax.rem(lax.broadcasted_iota(jnp.int32, (mband, width), 0), mid)
    column = jnp.zeros((mband, width), jnp.float32)
    for o in range(mid):
        column = jnp.where(which == o, bias_ref[0, o], column)
    bias[...] = column

    def weight_of(s):
        return mask_ref[0, s].astype(jnp.float32)

    count = 1.0 + weight_of(0) + weight_of(1) + weight_of(2) + weight_of(3)
    inv = 1.0 / jnp.full((1, width), count, jnp.float32)

    arrivals = []
    for n, (src, dst) in enumerate(
        [(ints_in, ints), (ints_in, ints), (floats_in, floats), (floats_in, floats)]
    ):
        scalar_copies[n].wait_recv()
        arrivals.append(pltpu.make_async_copy(src.at[n % 2], dst.at[other, n % 2], local_sem.at[10 + n]))
        arrivals[-1].start()
    halo_copy.wait_recv()
    for i in range(2):
        shift_plane(halo[i * mband : (i + 1) * mband, :], own * other + i)
    for arrival in arrivals:
        arrival.wait()

    def place(p):
        at_plane = p + me * (2 * own - planes)
        return at_plane // own, lax.rem(at_plane, own)

    def row_of(s, p):
        slab, lane = place(p)
        return ints[slab, 0, s, lane]

    def weights(s, p):
        slab, lane = place(p)
        c = ints[slab, 1, s, lane]
        fy = floats[slab, 0, s, lane]
        fx = floats[slab, 1, s, lane]
        spot = lanes(width) + c
        left = jnp.where((spot >= 0) & (spot < width), 1.0 - fx, 0.0)
        right = jnp.where((spot >= -1) & (spot < width - 1), fx, 0.0)
        return c, fy, left, right

    def warp_slot(t, last):
        s = slot(t)

        def plane(p, _):
            c, fy, left, right = weights(s, p)
            r = row_of(s, p)
            window = bands[t, : band + chans, :]
            for k in range(1, lead + 1):
                window = jnp.where(r == k, bands[t, k * chans : band + (k + 1) * chans, :], window)
            here = turned(window, c)
            for h in range(height):
                rows = slice(h * chans, (h + 1) * chans)
                mixed = (1.0 - fy) * here[rows] + fy * here[(h + 1) * chans : (h + 2) * chans]
                warped = left * mixed + right * pltpu.roll(mixed, width - 1, 1)
                warp[t, p, rows, :] = warped
                if last:
                    ref = feat_ref[(top + h) * chans : (top + h + 1) * chans, :].astype(jnp.float32)
                    first = ref
                    second = ref * ref
                    for u in range(4):
                        view = warped if u == t else warp[u, p, rows, :]
                        weighted = weight_of(slot(u)) * view
                        first = first + weighted
                        second = second + weighted * view
                    average = first * inv
                    mean[p, rows, :] = average
                    spot = pl.multiple_of((p + 1) * band + h * chans, chans)
                    cost[pl.ds(spot, chans), :] = (second * inv - average * average).astype(cost.dtype)
            return 0

        in_steps(planes, 3, plane)

    feat2.wait_recv()
    warp_slot(2, False)
    feat1.wait_recv()
    over1 = begin(remote(14, part(bands.at[1], me), part(bands.at[1], me), (cam, other)))
    feat3 = begin(remote(6, part(bands.at[1], me), part(bands.at[3], me), (mate, me)))
    feat0.wait_recv()
    over0 = begin(remote(15, part(bands.at[0], me), part(bands.at[0], me), (cam, other)))
    over1.wait_recv()
    over3 = begin(remote(16, part(bands.at[1], other), part(bands.at[3], other), (mate, me)))
    warp_slot(1, False)
    feat3.wait_recv()
    over3.wait_recv()
    warp_slot(3, False)
    over0.wait_recv()
    warp_slot(0, True)

    def middle(i, _):
        p = first_own // 2 + i
        x = cost[pl.ds(pl.multiple_of(p * band, band), 3 * band), :]
        parts = mul(b1_ref[...], x)
        pre = from_left(parts[:mband]) + parts[mband : 2 * mband] + from_right(parts[2 * mband :])
        pre = pre + bias[...]
        gate = jax.nn.sigmoid(pre)
        hid[pl.ds(pl.multiple_of(p * mband, mband), mband), :] = (pre * gate).astype(hid.dtype)
        y = scot[pl.ds(pl.multiple_of(p * 3 * mband, 3 * mband), 3 * 3 * mband), :]
        back = mul(b2_ref[:, : 9 * mband], y) * (gate * (1.0 + pre * (1.0 - gate)))
        base = pl.multiple_of((p + 1) * 3 * mband, mband)
        spre[pl.ds(base, mband), :] = from_left(back).astype(spre.dtype)
        spre[pl.ds(base + mband, mband), :] = back.astype(spre.dtype)
        spre[pl.ds(base + 2 * mband, mband), :] = from_right(back).astype(spre.dtype)
        return 0

    in_steps(own + (planes - own) // 2, own + (planes - own) // 2, middle)

    acc1[...] = jnp.zeros_like(acc1)
    acc2[...] = jnp.zeros_like(acc2)
    own_grad[...] = jnp.zeros_like(own_grad)

    def back_plane(i, _):
        p = first_own + i
        s3 = spre[pl.ds(pl.multiple_of(p * 3 * mband, 3 * mband), 9 * mband), :]
        c3 = scot[pl.ds(pl.multiple_of(p * 3 * mband, 3 * mband), 9 * mband), :]
        cg[i] = mul(b3_ref[:, : 9 * mband], s3) * (2.0 * inv)
        acc1[...] += mul_t(s3, cost[pl.ds(pl.multiple_of((p + 1) * band, band), band), :])
        acc2[:, :mband] += mul_t(c3, hid[pl.ds(pl.multiple_of(p * mband, mband), mband), :])
        return 0

    in_steps(own, 4, back_plane)

    def fold(acc, block, offset):
        rows = acc[...].reshape(9, height, mid, 128)
        lane = lax.broadcasted_iota(jnp.int32, (1, 1, 128), 2)
        total = None
        for g in range(height):
            ok = (lane >= (g - 1) * block) & (lane < (g + 2) * block) & (lane < height * block)
            part = jnp.where(ok, rows[:, g], 0.0).reshape(9 * mid, 128)
            turn = (offset - (g - 1) * block) % 128
            if turn:
                part = pltpu.roll(part, turn, 1)
            total = part if total is None else total + part
        return total

    ar[0] = fold(acc1, chans, 0) + fold(acc2, mid, 3 * chans)
    reduce_copies = []

    def reduce_begin():
        k = len(reduce_copies)
        if k < steps:
            reduce_copies.append(begin(remote(19 + k, ar.at[k], ar_in.at[k], partners[k])))

    def reduce_next():
        k = len(reduce_copies)
        if k <= steps and k > 0:
            reduce_copies[k - 1].wait_recv()
            ar[k] = ar[k - 1] + ar_in[k - 1]

    reduce_begin()

    def slot_back(t, emit):
        s = slot(t)
        weight = weight_of(s)

        def plane(i, _):
            p = first_own + i
            c, fy, left, right = weights(s, p)
            carried = None
            for h in range(height):
                rows = slice(h * chans, (h + 1) * chans)
                grad = (weight * cg[i, rows, :]) * (warp[t, p, rows, :] - mean[p, rows, :])
                taps[rows, :] = (left * grad + pltpu.roll(right * grad, 1, 1)).astype(taps.dtype)
            spread = turned(taps[...], -c)
            for h in range(height):
                rows = slice(h * chans, (h + 1) * chans)
                value = (1.0 - fy) * spread[rows]
                if carried is not None:
                    value = value + carried
                carried = fy * spread[rows]
                pad[i, rows, :] = value
            pad[i, height * chans :, :] = carried
            return 0

        in_steps(own, 4, plane)
        starts = [row_of(s, first_own + i) for i in range(own)]
        for r in range(held):
            total = None
            for i in range(own):
                part = jnp.zeros((chans, width), pad.dtype)
                for k in range(lead + 1):
                    if 0 <= r - k <= height:
                        row = pad[i, (r - k) * chans : (r - k + 1) * chans, :]
                        part = jnp.where(starts[i] == k, row, part)
                total = part if total is None else total + part
            for e in range(2):
                emit(e, slice(r * half, (r + 1) * half), total[e * half : (e + 1) * half])

    def to_mate(n):
        def emit(e, rows, value):
            a_send[n, e, rows, :] = value.astype(a_send.dtype)

        return emit

    def outward(n):
        def emit(e, rows, value):
            out_grad[n, e, rows, :] = value

        return emit

    slot_back(3, to_mate(1))
    a1 = begin(remote(8, a_send.at[1], a_recv.at[1], (mate, me)))
    reduce_next()
    reduce_begin()
    slot_back(0, outward(0))
    b_send[0] = out_grad[0, other].astype(b_send.dtype)
    b0 = begin(remote(9, b_send.at[0], b_recv.at[0], (cam, other)))
    reduce_next()
    reduce_begin()
    slot_back(1, outward(1))
    a1.wait_recv()
    b_send[1] = (out_grad[1, other] + a_recv[1, other].astype(jnp.float32)).astype(b_send.dtype)
    b1 = begin(remote(10, b_send.at[1], b_recv.at[1], (cam, other)))
    b0.wait_recv()
    c_send[0] = (out_grad[0, me] + b_recv[0].astype(jnp.float32)).astype(c_send.dtype)
    c0 = begin(remote(12, c_send.at[0], c_recv.at[0], (at(2), me)))
    reduce_next()
    reduce_begin()
    slot_back(2, to_mate(0))
    a0 = begin(remote(7, a_send.at[0], a_recv.at[0], (mate, me)))
    b1.wait_recv()
    c_send[1] = (
        out_grad[1, me] + a_recv[1, me].astype(jnp.float32) + b_recv[1].astype(jnp.float32)
    ).astype(c_send.dtype)
    c1 = begin(remote(13, c_send.at[1], c_recv.at[1], (at(1), me)))
    reduce_next()
    reduce_begin()

    for h in range(height):
        rows = slice(h * chans, (h + 1) * chans)
        ref = feat_ref[(top + h) * chans : (top + h + 1) * chans, :].astype(jnp.float32)
        total = None
        for i in range(own):
            term = cg[i, rows, :] * (ref - mean[first_own + i, rows, :])
            total = term if total is None else total + term
        for e in range(2):
            own_grad[e, (top + h) * half : (top + h + 1) * half, :] = total[e * half : (e + 1) * half]
    a0.wait_recv()
    b_send[2] = (own_grad[other] + a_recv[0, other].astype(jnp.float32)).astype(b_send.dtype)
    b2 = begin(remote(11, b_send.at[2], b_recv.at[2], (cam, other)))
    while len(reduce_copies) < steps:
        reduce_next()
        reduce_begin()
    reduce_next()
    wsum_ref[...] = ar[steps]
    b2.wait_recv()
    own_grad[me] = own_grad[me] + a_recv[0, me].astype(jnp.float32) + b_recv[2].astype(jnp.float32)
    c0.wait_recv()
    c1.wait_recv()
    grad_ref[...] = own_grad[me] + (c_recv[0].astype(jnp.float32) + c_recv[1].astype(jnp.float32))
    for copy in started:
        copy.wait_send()


def shards(
    features, view_mask, row_offset, frac_row, col_offset, frac_col,
    first_kernel, first_bias, second_kernel, cotangent,
):
    cams, slabs = lax.axis_size("cam"), lax.axis_size("depth")
    _, chans, held, width = features.shape
    mid = first_kernel.shape[0]
    _, _, own, height, _ = cotangent.shape
    band, mband, half = height * chans, height * mid, chans // 2
    assert slabs == 2 and 2 <= own <= 64 and band == 128 and width % 256 == 0 and cams & (cams - 1) == 0
    planes = own + 2
    steps = cams.bit_length()

    order = (2, 3, 4, 0, 1)
    w1 = jnp.transpose(first_kernel, order)
    w2 = jnp.transpose(second_kernel, order)

    f32, bf16, i32 = jnp.float32, jnp.bfloat16, jnp.int32
    rows = held * half
    taps_rows = -(-9 * mband // 128) * 128
    grads, wsum = pl.pallas_call(
        functools.partial(compute, (chans, mid, height, held, width, own, planes, cams)),
        out_shape=(
            jax.ShapeDtypeStruct((rows, width), f32),
            jax.ShapeDtypeStruct((9 * mid, 128), f32),
        ),
        in_specs=[HBM] * 10,
        out_specs=(VMEM, VMEM),
        scratch_shapes=[
            pltpu.VMEM(features.shape[1:], bf16),
            pltpu.VMEM(cotangent.shape[1:], bf16),
            pltpu.SMEM((1, 4), i32),
            pltpu.SMEM((1, mid), f32),
            pltpu.VMEM(w1.shape, bf16),
            pltpu.VMEM(w2.shape, bf16),
            pltpu.VMEM((4, held * chans, width), bf16),
            pltpu.VMEM((2 * mband, width), bf16),
            pltpu.VMEM((2, 4, own), i32),
            pltpu.VMEM((2, 4, own), f32),
            pltpu.SMEM((2, 2, 4, own), i32),
            pltpu.SMEM((2, 2, 4, own), f32),
            pltpu.VMEM((4, planes, band, width), f32),
            pltpu.VMEM((planes, band, width), f32),
            pltpu.VMEM(((planes + 2) * band, width), bf16),
            pltpu.VMEM(((planes + 2) * 3 * mband, width), bf16),
            pltpu.VMEM(((planes + 2) * 3 * mband, width), bf16),
            pltpu.VMEM((planes * mband, width), bf16),
            pltpu.VMEM((9 * mband, 128), f32),
            pltpu.VMEM((9 * mband, 128), f32),
            pltpu.VMEM((own, band, width), f32),
            pltpu.VMEM((own, band + chans, width), f32),
            pltpu.VMEM((band, width), bf16),
            pltpu.VMEM((2, rows, width), f32),
            pltpu.VMEM((2, 2, rows, width), f32),
            pltpu.VMEM((2, 2, rows, width), bf16),
            pltpu.VMEM((2, 2, rows, width), bf16),
            pltpu.VMEM((3, rows, width), bf16),
            pltpu.VMEM((3, rows, width), bf16),
            pltpu.VMEM((2, rows, width), bf16),
            pltpu.VMEM((2, rows, width), bf16),
            pltpu.VMEM((steps + 1, 9 * mid, 128), f32),
            pltpu.VMEM((steps, 9 * mid, 128), f32),
            pltpu.VMEM((chans, held, width), f32),
            pltpu.VMEM((mid, own * height, width), f32),
            pltpu.VMEM((held * chans, width), bf16),
            pltpu.VMEM((own * mband, width), bf16),
            pltpu.VMEM((3 * mband, 3 * band), bf16),
            pltpu.VMEM((3 * mband, 3 * band), f32),
            pltpu.VMEM((mband, taps_rows), bf16),
            pltpu.VMEM((taps_rows, 128), f32),
            pltpu.VMEM((band, taps_rows), bf16),
            pltpu.VMEM((taps_rows, 128), f32),
            pltpu.VMEM((mband, width), f32),
            pltpu.SemaphoreType.DMA((19 + steps,)),
            pltpu.SemaphoreType.DMA((19 + steps,)),
            pltpu.SemaphoreType.DMA((14,)),
        ],
        compiler_params=pltpu.CompilerParams(
            vmem_limit_bytes=62 * 2**20, collective_id=0, has_side_effects=True
        ),
        name="core",
    )(
        features[0], cotangent[0], row_offset[0], col_offset[0], frac_row[0], frac_col[0],
        view_mask, first_bias[None], w1, w2,
    )

    feature_grad = jnp.transpose(grads.reshape(held, half, width), (1, 0, 2))
    scale = (cams * slabs * own * height * width) ** (-0.5)
    taps = (wsum * scale).reshape(3, 3, mid, 128)[::-1, ::-1]
    first = taps[..., : 3 * chans].reshape(3, 3, mid, 3, chans)
    second = taps[..., 3 * chans : 3 * chans + 3 * mid].reshape(3, 3, mid, 3, mid)
    order = (2, 4, 0, 3, 1)
    return feature_grad[None], jnp.transpose(first, order), jnp.transpose(second, order)


def solution(mesh):
    placed = (
        P("cam", None, None, None),
        P("cam", None),
        P("cam", None, "depth"),
        P("cam", None, "depth"),
        P("cam", None, "depth"),
        P("cam", None, "depth"),
        P(),
        P(),
        P(),
        P("cam", None, "depth", None, None),
    )
    return jax.shard_map(
        shards,
        mesh=mesh,
        in_specs=placed,
        out_specs=(P("cam", "depth", None, None), P(), P()),
        check_vma=False,
    )
```

```python
import functools

import jax
import jax.numpy as jnp
from jax import lax
from jax.experimental import pallas as pl
from jax.experimental.pallas import tpu as pltpu
from jax.sharding import PartitionSpec as P

view_offsets = (-2, -1, 1, 2)
MESH = pl.DeviceIdType.MESH
HBM = pl.BlockSpec(memory_space=pltpu.HBM)
VMEM = pl.BlockSpec(memory_space=pltpu.VMEM)


def mul(a, b):
    return jnp.dot(a, b, preferred_element_type=jnp.float32)


def mul_t(a, b):
    return lax.dot_general(a, b, (((1,), (1,)), ((), ())), preferred_element_type=jnp.float32)


def lanes(width):
    return lax.broadcasted_iota(jnp.int32, (1, width), 1)


def from_left(x):
    width = x.shape[1]
    return jnp.where(lanes(width) > 0, pltpu.roll(x, 1, 1), 0.0)


def from_right(x):
    width = x.shape[1]
    return jnp.where(lanes(width) < width - 1, pltpu.roll(x, width - 1, 1), 0.0)


def turned(x, by):
    count, width = x.shape
    parts = []
    for start in range(0, width, 256):
        before = (start - 128) % width
        after = (start + 256) % width
        parts.append(
            jnp.concatenate(
                [x[:, before : before + 128], x[:, start : start + 256], x[:, after : after + 128]], axis=1
            )
        )
    apart = lax.broadcasted_iota(jnp.int32, (128, 128), 0) - lax.broadcasted_iota(jnp.int32, (128, 128), 1)
    low, mid, high = (jnp.where(apart == by - d, 1.0, 0.0).astype(x.dtype) for d in (-128, 0, 128))
    none = jnp.zeros_like(mid)
    pick = jnp.concatenate(
        [jnp.concatenate([low, mid, high, none], axis=0), jnp.concatenate([none, low, mid, high], axis=0)], axis=1
    )
    out = mul(jnp.concatenate(parts, axis=0), pick)
    return jnp.concatenate([out[i * count : (i + 1) * count] for i in range(width // 256)], axis=1)


def in_steps(count, size, body):
    if count % size:
        size = 1

    def step(i, _):
        for n in range(size):
            body(i * size + n, 0)
        return 0

    if count == size:
        step(0, 0)
    else:
        lax.fori_loop(0, count // size, step, 0)


def compute(
    dims,
    raw_hbm, cotangent_hbm, row_hbm, col_hbm, fy_hbm, fx_hbm, mask_hbm, bias_hbm, w1_hbm, w2_hbm,
    grad_ref, wsum_ref,
    raw_ref, cotangent_ref, mask_ref, bias_ref, w1_ref, w2_ref,
    bands, halo, ints_in, floats_in, ints, floats,
    warp, mean, cost, scot, spre, hid, acc1, acc2, cg, pad, taps,
    own_grad, out_grad, a_send, a_recv, b_send, b_recv, c_send, c_recv, ar, ar_in,
    wide, cot_wide, feat_ref, cot_ref, b1_ref, b1_wide, b2_ref, b2_wide, b3_ref, b3_wide, bias,
    send_sem, recv_sem, local_sem,
):
    chans, mid, height, held, width, own, planes, cams = dims
    top = (held - height) // 2
    lead = held - height - 1
    half = chans // 2
    band = height * chans
    mband = height * mid
    steps = ar_in.shape[0]

    cam = lax.axis_index("cam")
    me = lax.axis_index("depth")
    other = 1 - me
    first_own = (planes - own) * me
    odd = lax.rem(cam, 2)

    def at(offset):
        return lax.rem(cam + cams + offset * (2 * odd - 1), cams)

    def slot(t):
        return t + odd * (3 - 2 * t)

    mate = at(-1)
    partners = []
    reach = 1
    while reach < cams:
        bit = lax.rem(cam // reach, 2)
        partners.append((cam + reach * (1 - 2 * bit), me))
        reach *= 2
    partners.append((cam, other))

    fetches = [
        pltpu.make_async_copy(src, dst, local_sem.at[n])
        for n, (src, dst) in enumerate(
            [
                (raw_hbm, raw_ref), (cotangent_hbm, cotangent_ref), (w1_hbm, w1_ref), (w2_hbm, w2_ref),
                (row_hbm, ints.at[me, 0]), (col_hbm, ints.at[me, 1]),
                (fy_hbm, floats.at[me, 0]), (fx_hbm, floats.at[me, 1]),
                (mask_hbm, mask_ref), (bias_hbm, bias_ref),
            ]
        )
    ]
    for fetch in fetches:
        fetch.start()

    barrier = pltpu.get_barrier_semaphore()
    greeted = [(at(-2), me), (at(-1), me), (at(1), me), (at(2), me)] + partners
    for device in greeted:
        pl.semaphore_signal(barrier, inc=1, device_id=device, device_id_type=MESH)

    fetches[0].wait()
    wide[...] = raw_ref[...].astype(jnp.float32)
    for r in range(held):
        feat_ref[r * chans : (r + 1) * chans, :] = wide[:, r, :].astype(feat_ref.dtype)

    pl.semaphore_wait(barrier, len(greeted))

    started = []

    def remote(n, src, dst, device):
        return pltpu.make_async_remote_copy(
            src_ref=src, dst_ref=dst, send_sem=send_sem.at[n], recv_sem=recv_sem.at[n],
            device_id=device, device_id_type=MESH,
        )

    def begin(copy):
        copy.start()
        started.append(copy)
        return copy

    span = held // 2 * chans

    def part(ref, e):
        return ref.at[pl.ds(pl.multiple_of(e * span, span), span), :]

    feat1 = begin(remote(4, part(feat_ref, me), part(bands.at[1], me), (at(1), me)))
    feat0 = begin(remote(3, part(feat_ref, me), part(bands.at[0], me), (at(-2), me)))
    feat2 = begin(remote(5, feat_ref, bands.at[2], (mate, me)))
    scalar_copies = [
        begin(remote(n, src, dst, (cam, other)))
        for n, src, dst in (
            (0, row_hbm, ints_in.at[0]), (1, col_hbm, ints_in.at[1]),
            (17, fy_hbm, floats_in.at[0]), (18, fx_hbm, floats_in.at[1]),
        )
    ]

    fetches[1].wait()
    for i in range(own):
        cot_wide[:, i * height : (i + 1) * height, :] = cotangent_ref[:, i].astype(jnp.float32)
    for i in range(own):
        cot_ref[i * mband : (i + 1) * mband, :] = jnp.concatenate(
            [cot_wide[:, i * height + h, :] for h in range(height)], axis=0
        ).astype(cot_ref.dtype)
    edge = pl.multiple_of((own - 2) * other * mband, mband)
    halo_copy = begin(remote(2, cot_ref.at[pl.ds(edge, 2 * mband), :], halo, (cam, other)))

    for end in (0, planes + 1):
        scot[end * 3 * mband : (end + 1) * 3 * mband, :] = jnp.zeros((3 * mband, width), scot.dtype)
        spre[end * 3 * mband : (end + 1) * 3 * mband, :] = jnp.zeros((3 * mband, width), spre.dtype)
        cost[end * band : (end + 1) * band, :] = jnp.zeros((band, width), cost.dtype)

    def shift_plane(plane, p):
        wide = plane.astype(jnp.float32)
        base = pl.multiple_of((p + 1) * 3 * mband, mband)
        scot[pl.ds(base, mband), :] = from_left(wide).astype(scot.dtype)
        scot[pl.ds(base + mband, mband), :] = plane
        scot[pl.ds(base + 2 * mband, mband), :] = from_right(wide).astype(scot.dtype)

    for i in range(own):
        shift_plane(cot_ref[i * mband : (i + 1) * mband, :], first_own + i)

    def blocks(w_ref, block, kd, kw):
        taps = []
        for kh in range(3):
            tap = w_ref[kd, kh, kw].astype(jnp.float32)
            taps.append(jnp.concatenate([tap, jnp.zeros((mid, 128 - block), jnp.float32)], axis=1))
        found = []
        for h in range(height):
            total = None
            for kh in range(3):
                to = h + kh - 1
                if 0 <= to < height:
                    moved = taps[kh] if to == 0 else pltpu.roll(taps[kh], to * block, 1)
                    total = moved if total is None else total + moved
            found.append(total)
        return found

    for fetch in fetches[2:]:
        fetch.wait()
    for kd in range(3):
        for kw in range(3):
            for h, value in enumerate(blocks(w1_ref, chans, kd, kw)):
                row = (kw * height + h) * mid
                b1_wide[row : row + mid, kd * 128 : (kd + 1) * 128] = value
                row = (((2 - kd) * 3 + 2 - kw) * height + h) * mid
                b3_wide[row : row + mid, :] = value
            for h, value in enumerate(blocks(w2_ref, mid, kd, kw)):
                row = (((2 - kd) * 3 + 2 - kw) * height + h) * mid
                b2_wide[row : row + mid, :] = value
    for ref in (b2_wide, b3_wide):
        ref[9 * mband :, :] = jnp.zeros((ref.shape[0] - 9 * mband, 128), jnp.float32)
    b1_ref[...] = b1_wide[...].astype(b1_ref.dtype)
    b2_ref[...] = jnp.transpose(b2_wide[...])[:mband].astype(b2_ref.dtype)
    b3_ref[...] = jnp.transpose(b3_wide[...]).astype(b3_ref.dtype)
    which = lax.rem(lax.broadcasted_iota(jnp.int32, (mband, width), 0), mid)
    column = jnp.zeros((mband, width), jnp.float32)
    for o in range(mid):
        column = jnp.where(which == o, bias_ref[0, o], column)
    bias[...] = column

    def weight_of(s):
        return mask_ref[0, s].astype(jnp.float32)

    count = 1.0 + weight_of(0) + weight_of(1) + weight_of(2) + weight_of(3)
    inv = 1.0 / jnp.full((1, width), count, jnp.float32)

    arrivals = []
    for n, (src, dst) in enumerate(
        [(ints_in, ints), (ints_in, ints), (floats_in, floats), (floats_in, floats)]
    ):
        scalar_copies[n].wait_recv()
        arrivals.append(pltpu.make_async_copy(src.at[n % 2], dst.at[other, n % 2], local_sem.at[10 + n]))
        arrivals[-1].start()
    halo_copy.wait_recv()
    for i in range(2):
        shift_plane(halo[i * mband : (i + 1) * mband, :], own * other + i)
    for arrival in arrivals:
        arrival.wait()

    def place(p):
        at_plane = p + me * (2 * own - planes)
        return at_plane // own, lax.rem(at_plane, own)

    def row_of(s, p):
        slab, lane = place(p)
        return ints[slab, 0, s, lane]

    def weights(s, p):
        slab, lane = place(p)
        c = ints[slab, 1, s, lane]
        fy = floats[slab, 0, s, lane]
        fx = floats[slab, 1, s, lane]
        spot = lanes(width) + c
        left = jnp.where((spot >= 0) & (spot < width), 1.0 - fx, 0.0)
        right = jnp.where((spot >= -1) & (spot < width - 1), fx, 0.0)
        return c, fy, left, right

    def warp_slot(t, last):
        s = slot(t)

        def plane(p, _):
            c, fy, left, right = weights(s, p)
            r = row_of(s, p)
            window = bands[t, : band + chans, :]
            for k in range(1, lead + 1):
                window = jnp.where(r == k, bands[t, k * chans : band + (k + 1) * chans, :], window)
            here = turned(window, c)
            for h in range(height):
                rows = slice(h * chans, (h + 1) * chans)
                mixed = (1.0 - fy) * here[rows] + fy * here[(h + 1) * chans : (h + 2) * chans]
                warped = left * mixed + right * pltpu.roll(mixed, width - 1, 1)
                warp[t, p, rows, :] = warped
                if last:
                    ref = feat_ref[(top + h) * chans : (top + h + 1) * chans, :].astype(jnp.float32)
                    first = ref
                    second = ref * ref
                    for u in range(4):
                        view = warped if u == t else warp[u, p, rows, :]
                        weighted = weight_of(slot(u)) * view
                        first = first + weighted
                        second = second + weighted * view
                    average = first * inv
                    mean[p, rows, :] = average
                    spot = pl.multiple_of((p + 1) * band + h * chans, chans)
                    cost[pl.ds(spot, chans), :] = (second * inv - average * average).astype(cost.dtype)
            return 0

        in_steps(planes, 3, plane)

    feat2.wait_recv()
    warp_slot(2, False)
    feat1.wait_recv()
    over1 = begin(remote(14, part(bands.at[1], me), part(bands.at[1], me), (cam, other)))
    feat3 = begin(remote(6, part(bands.at[1], me), part(bands.at[3], me), (mate, me)))
    feat0.wait_recv()
    over0 = begin(remote(15, part(bands.at[0], me), part(bands.at[0], me), (cam, other)))
    over1.wait_recv()
    over3 = begin(remote(16, part(bands.at[1], other), part(bands.at[3], other), (mate, me)))
    warp_slot(1, False)
    feat3.wait_recv()
    over3.wait_recv()
    warp_slot(3, False)
    over0.wait_recv()
    warp_slot(0, True)

    def middle(i, _):
        p = first_own // 2 + i
        x = cost[pl.ds(pl.multiple_of(p * band, band), 3 * band), :]
        parts = mul(b1_ref[...], x)
        pre = from_left(parts[:mband]) + parts[mband : 2 * mband] + from_right(parts[2 * mband :])
        pre = pre + bias[...]
        gate = jax.nn.sigmoid(pre)
        hid[pl.ds(pl.multiple_of(p * mband, mband), mband), :] = (pre * gate).astype(hid.dtype)
        y = scot[pl.ds(pl.multiple_of(p * 3 * mband, 3 * mband), 3 * 3 * mband), :]
        back = mul(b2_ref[:, : 9 * mband], y) * (gate * (1.0 + pre * (1.0 - gate)))
        base = pl.multiple_of((p + 1) * 3 * mband, mband)
        spre[pl.ds(base, mband), :] = from_left(back).astype(spre.dtype)
        spre[pl.ds(base + mband, mband), :] = back.astype(spre.dtype)
        spre[pl.ds(base + 2 * mband, mband), :] = from_right(back).astype(spre.dtype)
        return 0

    in_steps(own + (planes - own) // 2, own + (planes - own) // 2, middle)

    acc1[...] = jnp.zeros_like(acc1)
    acc2[...] = jnp.zeros_like(acc2)
    own_grad[...] = jnp.zeros_like(own_grad)

    def back_plane(i, _):
        p = first_own + i
        s3 = spre[pl.ds(pl.multiple_of(p * 3 * mband, 3 * mband), 9 * mband), :]
        c3 = scot[pl.ds(pl.multiple_of(p * 3 * mband, 3 * mband), 9 * mband), :]
        cg[i] = mul(b3_ref[:, : 9 * mband], s3) * (2.0 * inv)
        acc1[...] += mul_t(s3, cost[pl.ds(pl.multiple_of((p + 1) * band, band), band), :])
        acc2[:, :mband] += mul_t(c3, hid[pl.ds(pl.multiple_of(p * mband, mband), mband), :])
        return 0

    in_steps(own, 4, back_plane)

    def fold(acc, block, offset):
        rows = acc[...].reshape(9, height, mid, 128)
        lane = lax.broadcasted_iota(jnp.int32, (1, 1, 128), 2)
        total = None
        for g in range(height):
            ok = (lane >= (g - 1) * block) & (lane < (g + 2) * block) & (lane < height * block)
            part = jnp.where(ok, rows[:, g], 0.0).reshape(9 * mid, 128)
            turn = (offset - (g - 1) * block) % 128
            if turn:
                part = pltpu.roll(part, turn, 1)
            total = part if total is None else total + part
        return total

    ar[0] = fold(acc1, chans, 0) + fold(acc2, mid, 3 * chans)
    reduce_copies = []

    def reduce_begin():
        k = len(reduce_copies)
        if k < steps:
            reduce_copies.append(begin(remote(19 + k, ar.at[k], ar_in.at[k], partners[k])))

    def reduce_next():
        k = len(reduce_copies)
        if k <= steps and k > 0:
            reduce_copies[k - 1].wait_recv()
            ar[k] = ar[k - 1] + ar_in[k - 1]

    reduce_begin()

    def slot_back(t, emit):
        s = slot(t)
        weight = weight_of(s)

        def plane(i, _):
            p = first_own + i
            c, fy, left, right = weights(s, p)
            carried = None
            for h in range(height):
                rows = slice(h * chans, (h + 1) * chans)
                grad = (weight * cg[i, rows, :]) * (warp[t, p, rows, :] - mean[p, rows, :])
                taps[rows, :] = (left * grad + pltpu.roll(right * grad, 1, 1)).astype(taps.dtype)
            spread = turned(taps[...], -c)
            for h in range(height):
                rows = slice(h * chans, (h + 1) * chans)
                value = (1.0 - fy) * spread[rows]
                if carried is not None:
                    value = value + carried
                carried = fy * spread[rows]
                pad[i, rows, :] = value
            pad[i, height * chans :, :] = carried
            return 0

        in_steps(own, 4, plane)
        starts = [row_of(s, first_own + i) for i in range(own)]
        for r in range(held):
            total = None
            for i in range(own):
                part = jnp.zeros((chans, width), pad.dtype)
                for k in range(lead + 1):
                    if 0 <= r - k <= height:
                        row = pad[i, (r - k) * chans : (r - k + 1) * chans, :]
                        part = jnp.where(starts[i] == k, row, part)
                total = part if total is None else total + part
            for e in range(2):
                emit(e, slice(r * half, (r + 1) * half), total[e * half : (e + 1) * half])

    def to_mate(n):
        def emit(e, rows, value):
            a_send[n, e, rows, :] = value.astype(a_send.dtype)

        return emit

    def outward(n):
        def emit(e, rows, value):
            out_grad[n, e, rows, :] = value

        return emit

    slot_back(3, to_mate(1))
    a1 = begin(remote(8, a_send.at[1], a_recv.at[1], (mate, me)))
    reduce_next()
    reduce_begin()
    slot_back(0, outward(0))
    b_send[0] = out_grad[0, other].astype(b_send.dtype)
    b0 = begin(remote(9, b_send.at[0], b_recv.at[0], (cam, other)))
    reduce_next()
    reduce_begin()
    slot_back(1, outward(1))
    a1.wait_recv()
    b_send[1] = (out_grad[1, other] + a_recv[1, other].astype(jnp.float32)).astype(b_send.dtype)
    b1 = begin(remote(10, b_send.at[1], b_recv.at[1], (cam, other)))
    b0.wait_recv()
    c_send[0] = (out_grad[0, me] + b_recv[0].astype(jnp.float32)).astype(c_send.dtype)
    c0 = begin(remote(12, c_send.at[0], c_recv.at[0], (at(2), me)))
    reduce_next()
    reduce_begin()
    slot_back(2, to_mate(0))
    a0 = begin(remote(7, a_send.at[0], a_recv.at[0], (mate, me)))
    b1.wait_recv()
    c_send[1] = (
        out_grad[1, me] + a_recv[1, me].astype(jnp.float32) + b_recv[1].astype(jnp.float32)
    ).astype(c_send.dtype)
    c1 = begin(remote(13, c_send.at[1], c_recv.at[1], (at(1), me)))
    reduce_next()
    reduce_begin()

    for h in range(height):
        rows = slice(h * chans, (h + 1) * chans)
        ref = feat_ref[(top + h) * chans : (top + h + 1) * chans, :].astype(jnp.float32)
        total = None
        for i in range(own):
            term = cg[i, rows, :] * (ref - mean[first_own + i, rows, :])
            total = term if total is None else total + term
        for e in range(2):
            own_grad[e, (top + h) * half : (top + h + 1) * half, :] = total[e * half : (e + 1) * half]
    a0.wait_recv()
    b_send[2] = (own_grad[other] + a_recv[0, other].astype(jnp.float32)).astype(b_send.dtype)
    b2 = begin(remote(11, b_send.at[2], b_recv.at[2], (cam, other)))
    while len(reduce_copies) < steps:
        reduce_next()
        reduce_begin()
    reduce_next()
    wsum_ref[...] = ar[steps]
    b2.wait_recv()
    own_grad[me] = own_grad[me] + a_recv[0, me].astype(jnp.float32) + b_recv[2].astype(jnp.float32)
    c0.wait_recv()
    c1.wait_recv()
    for r in range(held):
        rows = slice(r * half, (r + 1) * half)
        landed = c_recv[0, rows, :].astype(jnp.float32) + c_recv[1, rows, :].astype(jnp.float32)
        grad_ref[:, r, :] = own_grad[me, rows, :] + landed
    for copy in started:
        copy.wait_send()


def shards(
    features, view_mask, row_offset, frac_row, col_offset, frac_col,
    first_kernel, first_bias, second_kernel, cotangent,
):
    cams, slabs = lax.axis_size("cam"), lax.axis_size("depth")
    _, chans, held, width = features.shape
    mid = first_kernel.shape[0]
    _, _, own, height, _ = cotangent.shape
    band, mband, half = height * chans, height * mid, chans // 2
    assert slabs == 2 and 2 <= own <= 64 and band == 128 and width % 256 == 0 and cams & (cams - 1) == 0
    planes = own + 2
    steps = cams.bit_length()

    order = (2, 3, 4, 0, 1)
    w1 = jnp.transpose(first_kernel, order)
    w2 = jnp.transpose(second_kernel, order)

    f32, bf16, i32 = jnp.float32, jnp.bfloat16, jnp.int32
    rows = held * half
    taps_rows = -(-9 * mband // 128) * 128
    grads, wsum = pl.pallas_call(
        functools.partial(compute, (chans, mid, height, held, width, own, planes, cams)),
        out_shape=(
            jax.ShapeDtypeStruct((half, held, width), f32),
            jax.ShapeDtypeStruct((9 * mid, 128), f32),
        ),
        in_specs=[HBM] * 10,
        out_specs=(VMEM, VMEM),
        scratch_shapes=[
            pltpu.VMEM(features.shape[1:], bf16),
            pltpu.VMEM(cotangent.shape[1:], bf16),
            pltpu.SMEM((1, 4), i32),
            pltpu.SMEM((1, mid), f32),
            pltpu.VMEM(w1.shape, bf16),
            pltpu.VMEM(w2.shape, bf16),
            pltpu.VMEM((4, held * chans, width), bf16),
            pltpu.VMEM((2 * mband, width), bf16),
            pltpu.VMEM((2, 4, own), i32),
            pltpu.VMEM((2, 4, own), f32),
            pltpu.SMEM((2, 2, 4, own), i32),
            pltpu.SMEM((2, 2, 4, own), f32),
            pltpu.VMEM((4, planes, band, width), f32),
            pltpu.VMEM((planes, band, width), f32),
            pltpu.VMEM(((planes + 2) * band, width), bf16),
            pltpu.VMEM(((planes + 2) * 3 * mband, width), bf16),
            pltpu.VMEM(((planes + 2) * 3 * mband, width), bf16),
            pltpu.VMEM((planes * mband, width), bf16),
            pltpu.VMEM((9 * mband, 128), f32),
            pltpu.VMEM((9 * mband, 128), f32),
            pltpu.VMEM((own, band, width), f32),
            pltpu.VMEM((own, band + chans, width), f32),
            pltpu.VMEM((band, width), bf16),
            pltpu.VMEM((2, rows, width), f32),
            pltpu.VMEM((2, 2, rows, width), f32),
            pltpu.VMEM((2, 2, rows, width), bf16),
            pltpu.VMEM((2, 2, rows, width), bf16),
            pltpu.VMEM((3, rows, width), bf16),
            pltpu.VMEM((3, rows, width), bf16),
            pltpu.VMEM((2, rows, width), bf16),
            pltpu.VMEM((2, rows, width), bf16),
            pltpu.VMEM((steps + 1, 9 * mid, 128), f32),
            pltpu.VMEM((steps, 9 * mid, 128), f32),
            pltpu.VMEM((chans, held, width), f32),
            pltpu.VMEM((mid, own * height, width), f32),
            pltpu.VMEM((held * chans, width), bf16),
            pltpu.VMEM((own * mband, width), bf16),
            pltpu.VMEM((3 * mband, 3 * band), bf16),
            pltpu.VMEM((3 * mband, 3 * band), f32),
            pltpu.VMEM((mband, taps_rows), bf16),
            pltpu.VMEM((taps_rows, 128), f32),
            pltpu.VMEM((band, taps_rows), bf16),
            pltpu.VMEM((taps_rows, 128), f32),
            pltpu.VMEM((mband, width), f32),
            pltpu.SemaphoreType.DMA((19 + steps,)),
            pltpu.SemaphoreType.DMA((19 + steps,)),
            pltpu.SemaphoreType.DMA((14,)),
        ],
        compiler_params=pltpu.CompilerParams(
            vmem_limit_bytes=62 * 2**20, collective_id=0, has_side_effects=True
        ),
        name="core",
    )(
        features[0], cotangent[0], row_offset[0], col_offset[0], frac_row[0], frac_col[0],
        view_mask, first_bias[None], w1, w2,
    )

    scale = (cams * slabs * own * height * width) ** (-0.5)
    taps = (wsum * scale).reshape(3, 3, mid, 128)[::-1, ::-1]
    first = taps[..., : 3 * chans].reshape(3, 3, mid, 3, chans)
    second = taps[..., 3 * chans : 3 * chans + 3 * mid].reshape(3, 3, mid, 3, mid)
    order = (2, 4, 0, 3, 1)
    return grads[None], jnp.transpose(first, order), jnp.transpose(second, order)


def solution(mesh):
    placed = (
        P("cam", None, None, None),
        P("cam", None),
        P("cam", None, "depth"),
        P("cam", None, "depth"),
        P("cam", None, "depth"),
        P("cam", None, "depth"),
        P(),
        P(),
        P(),
        P("cam", None, "depth", None, None),
    )
    return jax.shard_map(
        shards,
        mesh=mesh,
        in_specs=placed,
        out_specs=(P("cam", "depth", None, None), P(), P()),
        check_vma=False,
    )
```
